256 devices in a mesh: bond: 16 (over z, core), sec: 16 (over y, x).
Axes of the slice: x: 4, y: 4, z: 8, core: 2. Of those that a mesh axis runs over, the one named last changes fastest.
Arguments:
- left_site: bfloat16 [16, 64, 512, 512], P('bond', 'sec'), may hold values from -6 to 6
- right_site: bfloat16 [16, 64, 512, 512], P('bond', 'sec'), may hold values from -0.25 to 0.25
- gate: float32 [64, 64], replicated, may hold values from -2 to 2
- sign_table: int32 [64, 64], replicated, may hold values 0 or 1
- kept: int32 [16, 64], P('bond', 'sec'), may hold values from 32 to 128, as said below
- start: float32 [16, 64, 512, 128], P('bond', 'sec'), may hold values from -6 to 6
Outputs:
- left_new: bfloat16 [16, 64, 512, 128], P('bond', 'sec')
- right_new: bfloat16 [16, 64, 128, 512], P('bond', 'sec')
The draws below stay inside these ranges and needn't reach their ends.
Inputs may be any that keep to these rules, and one draw needn't show every extreme that they name: `kept`: kept counts are largest on the central bonds; sector 0 of bond 16 // 2 keeps 128.
All inputs are finite; a program needn't handle non-finite values.
Results may differ from the reference program's by a relative error of at most 0.011.
Values may be sent and summed in bfloat16 or wider, within the bound.
A program may use at most 64 MiB of HBM per device.

```python
import jax
import jax.numpy as jnp
from jax import lax

BLK = 512
KMAX = 128
SEC_DEV = 4
ITERS = 4
SECTORS = 64
BONDS = 16


def draw_kept(key, part):
    key = jax.random.fold_in(key, 7)
    position = jnp.arange(BONDS, dtype=jnp.int32)
    spread = jnp.abs(2 * position - (BONDS - 1))
    lowest = max(KMAX // 4, 1)
    ceiling = KMAX - KMAX // 2 * spread // max(BONDS - 1, 1)
    ceiling = jnp.maximum(ceiling, lowest)
    raw = jax.random.randint(key, (BONDS, SECTORS), 0, 1 << 20)
    counts = lowest + raw % (ceiling[:, None] - lowest + 1)
    counts = counts.at[BONDS // 2, 0].set(KMAX)
    return counts.astype(jnp.int32)


def plant(drawn, key, smallest, high):
    longest = drawn.shape.index(max(drawn.shape))
    spots = []
    for shift in (0, 1):
        where = [jax.random.randint(jax.random.fold_in(key, axis), (), 0, length) for axis, length in enumerate(drawn.shape)]
        where[longest] = (where[longest] + shift) % drawn.shape[longest]
        spots.append(tuple(where))
    return drawn.at[spots[0]].set(smallest).at[spots[1]].set(high)


def block_scale(key, shape, cuts, low, top_value):
    level = 1.0
    for dim, parts in cuts:
        steps = jax.random.uniform(jax.random.fold_in(jax.random.fold_in(key, 6), dim), (parts,), jnp.float32, low / len(cuts), top_value / len(cuts))
        level = level * jnp.repeat(jnp.exp(steps), shape[dim] // parts).reshape((-1,) + (1,) * (len(shape) - 1 - dim))
    return level


def scatter_about(key, dims, scale, bound, cuts=(), kind=jnp.bfloat16):
    result = scale * jax.random.normal(key, dims, jnp.float32)
    if cuts:
        result = result * block_scale(key, dims, cuts, -0.22, 0.18)
    return jnp.clip(result, -bound, bound).astype(kind)


def setup_inputs(seed: int = 0) -> dict:
    key_of = jax.random.split(jax.random.key(seed), 7)
    left_site = scatter_about(key_of[0], (BONDS, SECTORS, BLK, BLK), 1.0, 6.0, ((0, 16), (1, 16)))
    right_site = scatter_about(key_of[1], (BONDS, SECTORS, BLK, BLK), BLK ** -0.5, 0.25, ((0, 16), (1, 16)))
    gate = scatter_about(key_of[2], (SECTORS, SECTORS), 9 ** -0.5, 2.0, (), jnp.float32)
    sign_table = plant((jax.random.randint(key_of[3], (SECTORS, SECTORS), 0, 2) < 1).astype(jnp.int32), jax.random.fold_in(key_of[3], 1), 0, 1)
    kept = draw_kept(jax.random.fold_in(key_of[6], 71), 0)
    start = scatter_about(key_of[5], (BONDS, SECTORS, BLK, KMAX), 1.0, 6.0, ((0, 16), (1, 16)), jnp.float32)
    return dict(left_site=left_site, right_site=right_site, gate=gate, sign_table=sign_table, kept=kept, start=start)


def one_bond(items):
    left_block, right_block, basis, counts, coef = items
    pair = jnp.einsum('qij,qjk->qik', left_block.astype(jnp.float32), right_block.astype(jnp.float32)).astype(jnp.bfloat16)
    flat = pair.reshape(SECTORS, BLK * BLK).astype(jnp.float32)
    theta = jnp.dot(coef, flat, precision=lax.Precision.HIGHEST).astype(jnp.bfloat16).reshape(SECTORS, BLK, BLK)
    wide = theta.astype(jnp.float32)
    gram = jnp.einsum('pij,pkj->pik', wide, wide)
    for step in range(ITERS):
        grown = jnp.einsum('pij,pjk->pik', gram, basis, precision=lax.Precision.HIGHEST)
        inner = jnp.einsum('pji,pjk->pik', grown, grown, precision=lax.Precision.HIGHEST)
        factor = jnp.linalg.cholesky(inner)
        basis = lax.linalg.triangular_solve(factor, grown, left_side=False, lower=True, transpose_a=True)
    column = jnp.arange(KMAX, dtype=jnp.int32)
    masked = jnp.where(column[None, None, :] < counts[:, None, None], basis, jnp.float32(0.0))
    right = jnp.einsum('pik,pij->pkj', masked, wide, precision=lax.Precision.HIGHEST)
    return (masked.astype(jnp.bfloat16), right.astype(jnp.bfloat16))

def reference(left_site, right_site, gate, sign_table, kept, start):
    index = jnp.arange(SECTORS, dtype=jnp.int32)
    first = index // SEC_DEV
    second = index % SEC_DEV
    allowed = (jnp.abs(first[:, None] - first[None, :]) <= 1) & (jnp.abs(second[:, None] - second[None, :]) <= 1)
    coef = jnp.where(allowed, gate * (1.0 - 2.0 * sign_table.astype(jnp.float32)), jnp.float32(0.0))
    partner = jnp.roll(right_site, -1, axis=0)
    coefs = jnp.broadcast_to(coef, (BONDS, SECTORS, SECTORS))
    left_new, right_raw = lax.map(one_bond, (left_site, partner, start, kept, coefs))
    return (left_new, jnp.roll(right_raw, 1, axis=0))
```

```python
import functools
import jax
import jax.numpy as jnp
from jax import lax
from jax.experimental import pallas as pl
from jax.experimental.pallas import tpu as pltpu
from jax.sharding import PartitionSpec as P

ITERS=4
NB=16
F32=jnp.float32; BF=jnp.bfloat16

def split3(x):
    h=x.astype(BF)
    r=x-h.astype(F32)
    m=r.astype(BF)
    l=(r-m.astype(F32)).astype(BF)
    return h,m,l

def dot(a,b,ca,cb):
    return lax.dot_general(a,b,(((ca,),(cb,)),((),())),preferred_element_type=F32)

def dot6(a,b,ca,cb):
    ah,am,al=split3(a); bh,bm,bl=split3(b)
    return (dot(ah,bh,ca,cb)+(dot(ah,bm,ca,cb)+dot(am,bh,ca,cb))
            +(dot(ah,bl,ca,cb)+dot(am,bm,ca,cb)+dot(al,bh,ca,cb)))

def factor(aug, ubuf, tri, n, nb, S):
    for t in range(n//nb):
        lo=t*nb
        X=[aug[pl.ds(lo+k,2*S,stride=n),:] for k in range(nb)]
        v={}
        for i in range(nb):
            xa=jnp.concatenate([X[i][:S],X[i][:S]],axis=0)
            for k in range(i+1):
                v[i,k]=jnp.broadcast_to(xa[:,lo+k:lo+k+1],(2*S,n))
        U=[None]*nb
        for j in range(nb):
            r=lax.rsqrt(v[j,j])
            U[j]=X[j]*r
            tri[pl.ds(lo+j,S,stride=n),:]=U[j][S:]
            ubuf[pl.ds(j,2*S,stride=nb),:]=U[j]
            col={}
            for i in range(j+1,nb):
                col[i]=v[i,j]*r
            for i in range(j+1,nb):
                for k in range(j+1,i+1):
                    v[i,k]=v[i,k]-col[i]*col[k]
                X[i]=X[i]-col[i]*U[j]
        if lo+nb<n:
            for s in range(S):
                h,m,l=split3(ubuf[s*nb:(s+1)*nb,:])
                lhs=jnp.concatenate([h,h,m,h,m,l],axis=0)
                rhs=jnp.concatenate([h,m,h,l,m,h],axis=0)
                h,m,l=split3(ubuf[(S+s)*nb:(S+s+1)*nb,:])
                rhs2=jnp.concatenate([h,m,h,l,m,h],axis=0)
                up=dot(lhs,jnp.concatenate([rhs,rhs2],axis=1),0,0)
                rows=slice(s*n+lo+nb,(s+1)*n)
                aug[rows,:]=aug[rows,:]-up[lo+nb:,:n]
                rows=slice((S+s)*n+lo+nb,(S+s+1)*n)
                aug[rows,:]=aug[rows,:]-up[lo+nb:,n:]

def body(theta, start, kept, left, right, bt, gt, aug, ubuf, tri):
    S=theta.shape[0]; n=start.shape[2]; d=theta.shape[1]
    eye=(lax.broadcasted_iota(jnp.int32,(n,n),0)==lax.broadcasted_iota(jnp.int32,(n,n),1)).astype(F32)
    for s in range(S):
        bt[s]=start[s].T
    def it(_,c):
        for s in range(S):
            h,m,l=split3(bt[s])
            th=theta[s]
            z=dot(h,th,1,0)+(dot(m,th,1,0)+dot(l,th,1,0))
            h,m,l=split3(z)
            g=dot(h,th,1,1)+(dot(m,th,1,1)+dot(l,th,1,1))
            gt[s]=g
            aug[s*n:(s+1)*n,:]=dot6(g,g,1,1)
            aug[(S+s)*n:(S+s+1)*n,:]=eye
        factor(aug,ubuf,tri,n,NB,S)
        for s in range(S):
            bt[s]=dot6(tri[s*n:(s+1)*n,:],gt[s],1,0)
        return c
    lax.fori_loop(0,ITERS,it,0)
    for s in range(S):
        row=lax.broadcasted_iota(jnp.int32,(n,d),0)
        masked=jnp.where(row<kept[0,s],bt[s],0.0)
        left[s]=masked.T.astype(BF)
        h,m,l=split3(masked)
        th=theta[s]
        right[s]=(dot(h,th,1,0)+(dot(m,th,1,0)+dot(l,th,1,0))).astype(BF)

def subspace(theta,start,kept):
    S,d,_=theta.shape; n=start.shape[2]
    return pl.pallas_call(body,
        out_shape=(jax.ShapeDtypeStruct((S,d,n),BF),jax.ShapeDtypeStruct((S,n,d),BF)),
        in_specs=[pl.BlockSpec(memory_space=pltpu.VMEM),pl.BlockSpec(memory_space=pltpu.VMEM),pl.BlockSpec(memory_space=pltpu.SMEM)],
        out_specs=[pl.BlockSpec(memory_space=pltpu.VMEM)]*2,
        scratch_shapes=[pltpu.VMEM((S,n,d),F32),pltpu.VMEM((S,n,d),F32),pltpu.VMEM((2*S*n,n),F32),pltpu.VMEM((2*S*NB,n),F32),pltpu.VMEM((S*n,n),F32)],
        compiler_params=pltpu.CompilerParams(vmem_limit_bytes=40*2**20),
    )(theta,start,kept)


def shifted(value, axis, by):
    peers = lax.axis_size(axis)
    return lax.ppermute(value, axis, [(i, (i + by) % peers) for i in range(peers)])


def from_behind(value, axis, steps):
    count = lax.axis_size(axis)
    initial, last = (max(0, -steps), min(count, count - steps))
    return lax.ppermute(value, axis, [(source, source + steps) for source in range(initial, last)])


def shards(left_site, right_site, gate, sign_table, kept, start):
    sec_count = left_site.shape[1]
    sectors = gate.shape[0]
    sec_index = lax.axis_index("sec")
    coef = gate * (1.0 - 2.0 * sign_table.astype(jnp.float32))
    padded = jnp.pad(coef, ((0, 0), (sec_count, sec_count)))
    rows = lax.dynamic_slice_in_dim(padded, sec_index * sec_count, sec_count, 0)
    weights = lax.dynamic_slice_in_dim(rows, sec_index * sec_count, 3 * sec_count, 1)
    partner = shifted(right_site, "bond", -1)
    pair = jnp.einsum(
        "qij,qjk->qik", left_site[0], partner[0], preferred_element_type=jnp.float32
    ).astype(jnp.bfloat16)
    below = from_behind(pair, "sec", 1)
    above = from_behind(pair, "sec", -1)
    theta = []
    for p in range(sec_count):
        total = None
        for c, block in enumerate((below, pair, above)):
            for q in range(max(0, p - 1), min(sec_count, p + 2)):
                term = weights[p, c * sec_count + q] * block[q].astype(jnp.float32)
                total = term if total is None else total + term
        theta.append(total.astype(jnp.bfloat16))
    theta = jnp.stack(theta)
    left_new, right_local = subspace(theta, start[0], kept)
    return (left_new[None], shifted(right_local[None], "bond", 1))


def solution(mesh):
    return jax.shard_map(
        shards,
        mesh=mesh,
        in_specs=(
            P("bond", "sec", None, None),
            P("bond", "sec", None, None),
            P(),
            P(),
            P("bond", "sec"),
            P("bond", "sec", None, None),
        ),
        out_specs=(P("bond", "sec", None, None), P("bond", "sec", None, None)),
        check_vma=False,
    )
```

```python
import functools
import jax
import jax.numpy as jnp
from jax import lax
from jax.experimental import pallas as pl
from jax.experimental.pallas import tpu as pltpu
from jax.sharding import PartitionSpec as P

MESH = pl.DeviceIdType.MESH
ITERS=4
NB=16
F32=jnp.float32; BF=jnp.bfloat16

def split3(x):
    h=x.astype(BF)
    r=x-h.astype(F32)
    m=r.astype(BF)
    l=(r-m.astype(F32)).astype(BF)
    return h,m,l

def dot(a,b,ca,cb):
    return lax.dot_general(a,b,(((ca,),(cb,)),((),())),preferred_element_type=F32)

def dot6(a,b,ca,cb):
    ah,am,al=split3(a); bh,bm,bl=split3(b)
    return (dot(ah,bh,ca,cb)+(dot(ah,bm,ca,cb)+dot(am,bh,ca,cb))
            +(dot(ah,bl,ca,cb)+dot(am,bm,ca,cb)+dot(al,bh,ca,cb)))

def factor(aug, ubuf, tri, n, nb, S):
    for t in range(n//nb):
        lo=t*nb
        X=[aug[pl.ds(lo+k,2*S,stride=n),:] for k in range(nb)]
        v={}
        for i in range(nb):
            xa=jnp.concatenate([X[i][:S],X[i][:S]],axis=0)
            for k in range(i+1):
                v[i,k]=jnp.broadcast_to(xa[:,lo+k:lo+k+1],(2*S,n))
        U=[None]*nb
        for j in range(nb):
            r=lax.rsqrt(v[j,j])
            U[j]=X[j]*r
            tri[pl.ds(lo+j,S,stride=n),:]=U[j][S:]
            ubuf[pl.ds(j,2*S,stride=nb),:]=U[j]
            col={}
            for i in range(j+1,nb):
                col[i]=v[i,j]*r
            for i in range(j+1,nb):
                for k in range(j+1,i+1):
                    v[i,k]=v[i,k]-col[i]*col[k]
                X[i]=X[i]-col[i]*U[j]
        if lo+nb<n:
            for s in range(S):
                h,m,l=split3(ubuf[s*nb:(s+1)*nb,:])
                lhs=jnp.concatenate([h,h,m,h,m,l],axis=0)
                rhs=jnp.concatenate([h,m,h,l,m,h],axis=0)
                h,m,l=split3(ubuf[(S+s)*nb:(S+s+1)*nb,:])
                rhs2=jnp.concatenate([h,m,h,l,m,h],axis=0)
                up=dot(lhs,jnp.concatenate([rhs,rhs2],axis=1),0,0)
                rows=slice(s*n+lo+nb,(s+1)*n)
                aug[rows,:]=aug[rows,:]-up[lo+nb:,:n]
                rows=slice((S+s)*n+lo+nb,(S+s+1)*n)
                aug[rows,:]=aug[rows,:]-up[lo+nb:,n:]


def exchange_body(left, right, gate, sign, theta, left_v, partner, pair, below, above,
                  lsem, rs_sem, rr_sem, ps_sem, pr_sem):
    S, d, _ = left_v.shape
    bond, bonds = lax.axis_index("bond"), lax.axis_size("bond")
    f, nf = lax.axis_index("sec"), lax.axis_size("sec")
    ahead, behind = lax.rem(bond + 1, bonds), lax.rem(bond + bonds - 1, bonds)
    has_lo, has_hi = f > 0, f < nf - 1

    def load(q):
        return pltpu.make_async_copy(left.at[q], left_v.at[q], lsem.at[q])

    def shift(q):
        return pltpu.make_async_remote_copy(
            src_ref=right.at[q], dst_ref=partner.at[q], send_sem=rs_sem.at[q],
            recv_sem=rr_sem.at[q], device_id={"bond": behind}, device_id_type=MESH)

    def up(q):
        return pltpu.make_async_remote_copy(
            src_ref=pair.at[q], dst_ref=below.at[q], send_sem=ps_sem.at[0, q],
            recv_sem=pr_sem.at[0, q], device_id={"sec": f + 1}, device_id_type=MESH)

    def down(q):
        return pltpu.make_async_remote_copy(
            src_ref=pair.at[q], dst_ref=above.at[q], send_sem=ps_sem.at[1, q],
            recv_sem=pr_sem.at[1, q], device_id={"sec": f - 1}, device_id_type=MESH)

    for q in range(S):
        load(q).start()
    barrier = pltpu.get_barrier_semaphore()
    pl.semaphore_signal(barrier, inc=1, device_id={"bond": ahead}, device_id_type=MESH)
    pl.semaphore_signal(barrier, inc=1, device_id={"bond": behind}, device_id_type=MESH)

    @pl.when(has_lo)
    def _():
        pl.semaphore_signal(barrier, inc=1, device_id={"sec": f - 1}, device_id_type=MESH)

    @pl.when(has_hi)
    def _():
        pl.semaphore_signal(barrier, inc=1, device_id={"sec": f + 1}, device_id_type=MESH)

    pl.semaphore_wait(barrier, 2 + has_lo.astype(jnp.int32) + has_hi.astype(jnp.int32))

    for q in range(S):
        shift(q).start()

    @pl.when(jnp.logical_not(has_lo))
    def _():
        below[...] = jnp.zeros_like(below)

    @pl.when(jnp.logical_not(has_hi))
    def _():
        above[...] = jnp.zeros_like(above)

    def multiply(q, c):
        load(q).wait()
        shift(q).wait_recv()

        def rows(i, c):
            at = pl.ds(pl.multiple_of(i * 128, 128), 128)
            pair[q, at, :] = dot(left_v[q, at, :], partner[q], 1, 0).astype(BF)
            return c

        lax.fori_loop(0, d // 128, rows, 0)

        @pl.when(has_hi)
        def _():
            up(q).start()

        @pl.when(has_lo)
        def _():
            down(q).start()

        return c

    lax.fori_loop(0, S, multiply, 0)

    firsts = (jnp.maximum(f - 1, 0), f, jnp.minimum(f + 1, nf - 1))
    here = (has_lo.astype(F32), None, has_hi.astype(F32))

    def arrive(q):
        @pl.when(has_lo)
        def _():
            up(q).wait_recv()

        @pl.when(has_hi)
        def _():
            down(q).wait_recv()

    def mix(p):
        terms = []
        for first, gone, block in zip(firsts, here, (below, pair, above)):
            for q in range(max(0, p - 1), min(S, p + 2)):
                row, column = f * S + p, first * S + q
                w = gate[row, column] * (1.0 - 2.0 * sign[row, column].astype(F32))
                terms.append((w if gone is None else w * gone, block, q))

        def rows(i, c):
            at = pl.ds(pl.multiple_of(i * 16, 16), 16)
            total = None
            for w, block, q in terms:
                term = w * block[q, at, :].astype(F32)
                total = term if total is None else total + term
            theta[p, at, :] = total.astype(BF)
            return c

        lax.fori_loop(0, d // 16, rows, 0)

    arrive(0)
    arrive(1)
    mix(0)
    arrive(2)
    mix(1)
    arrive(3)
    mix(2)
    mix(3)
    for q in range(S):
        shift(q).wait_send()

        @pl.when(has_hi)
        def _():
            up(q).wait_send()

        @pl.when(has_lo)
        def _():
            down(q).wait_send()


def exchange(left, right, gate, sign):
    S, d, _ = left.shape
    block = pltpu.VMEM((S, d, d), BF)
    dma = pltpu.SemaphoreType.DMA
    hbm = pl.BlockSpec(memory_space=pl.ANY)
    smem = pl.BlockSpec(memory_space=pltpu.SMEM)
    return pl.pallas_call(
        exchange_body,
        out_shape=jax.ShapeDtypeStruct((S, d, d), BF),
        in_specs=[hbm, hbm, smem, smem],
        out_specs=pl.BlockSpec(memory_space=pltpu.VMEM),
        scratch_shapes=[block] * 5 + [dma((S,)), dma((S,)), dma((S,)), dma((2, S)), dma((2, S))],
        compiler_params=pltpu.CompilerParams(
            collective_id=0, has_side_effects=True, vmem_limit_bytes=24 * 2**20),
    )(left, right, gate, sign)


def iterate_body(theta, start, bt, gt, aug, ubuf, tri):
    S, d, n = start.shape
    eye = (lax.broadcasted_iota(jnp.int32, (n, n), 0)
           == lax.broadcasted_iota(jnp.int32, (n, n), 1)).astype(F32)
    for s in range(S):
        bt[s] = start[s].T

    def step(_, c):
        for s in range(S):
            th = theta[s]
            h, m, l = split3(bt[s])
            z = dot(h, th, 1, 0) + (dot(m, th, 1, 0) + dot(l, th, 1, 0))
            h, m, l = split3(z)
            g = dot(h, th, 1, 1) + (dot(m, th, 1, 1) + dot(l, th, 1, 1))
            gt[s] = g
            aug[s * n:(s + 1) * n, :] = dot6(g, g, 1, 1)
            aug[(S + s) * n:(S + s + 1) * n, :] = eye
        factor(aug, ubuf, tri, n, NB, S)
        for s in range(S):
            bt[s] = dot6(tri[s * n:(s + 1) * n, :], gt[s], 1, 0)
        return c

    lax.fori_loop(0, ITERS, step, 0)


def iterate(theta, start):
    S, d, n = start.shape
    vmem = pl.BlockSpec(memory_space=pltpu.VMEM)
    return pl.pallas_call(
        iterate_body,
        out_shape=jax.ShapeDtypeStruct((S, n, d), F32),
        in_specs=[vmem, vmem],
        out_specs=vmem,
        scratch_shapes=[
            pltpu.VMEM((S, n, d), F32),
            pltpu.VMEM((2 * S * n, n), F32),
            pltpu.VMEM((2 * S * NB, n), F32),
            pltpu.VMEM((S * n, n), F32),
        ],
        compiler_params=pltpu.CompilerParams(vmem_limit_bytes=24 * 2**20),
    )(theta, start)


def finish_body(theta, bt, kept, left_new, right_new, out, s_sem, r_sem):
    S, n, d = bt.shape
    bond, bonds = lax.axis_index("bond"), lax.axis_size("bond")
    ahead, behind = lax.rem(bond + 1, bonds), lax.rem(bond + bonds - 1, bonds)
    barrier = pltpu.get_barrier_semaphore()
    pl.semaphore_signal(barrier, inc=1, device_id={"bond": ahead}, device_id_type=MESH)
    pl.semaphore_signal(barrier, inc=1, device_id={"bond": behind}, device_id_type=MESH)
    row = lax.broadcasted_iota(jnp.int32, (n, d), 0)

    def back(s):
        return pltpu.make_async_remote_copy(
            src_ref=out.at[s], dst_ref=right_new.at[s], send_sem=s_sem.at[s],
            recv_sem=r_sem.at[s], device_id={"bond": ahead}, device_id_type=MESH)

    for s in range(S):
        masked = jnp.where(row < kept[0, s], bt[s], 0.0)
        h, m, l = split3(masked)
        th = theta[s]
        out[s] = (dot(h, th, 1, 0) + (dot(m, th, 1, 0) + dot(l, th, 1, 0))).astype(BF)
        if s == 0:
            pl.semaphore_wait(barrier, 2)
        back(s).start()
    for s in range(S):
        masked = jnp.where(row < kept[0, s], bt[s], 0.0)
        left_new[s] = masked.T.astype(BF)
    for s in range(S):
        back(s).wait()


def finish(theta, bt, kept):
    S, n, d = bt.shape
    vmem = pl.BlockSpec(memory_space=pltpu.VMEM)
    dma = pltpu.SemaphoreType.DMA
    return pl.pallas_call(
        finish_body,
        out_shape=(jax.ShapeDtypeStruct((S, d, n), BF), jax.ShapeDtypeStruct((S, n, d), BF)),
        in_specs=[vmem, vmem, pl.BlockSpec(memory_space=pltpu.SMEM)],
        out_specs=[vmem, pl.BlockSpec(memory_space=pl.ANY)],
        scratch_shapes=[pltpu.VMEM((S, n, d), BF), dma((S,)), dma((S,))],
        compiler_params=pltpu.CompilerParams(
            collective_id=1, has_side_effects=True, vmem_limit_bytes=24 * 2**20),
    )(theta, bt, kept)


def shards(left_site, right_site, gate, sign_table, kept, start):
    theta = exchange(left_site[0], right_site[0], gate, sign_table)
    bt = iterate(theta, start[0])
    left_new, right_new = finish(theta, bt, kept)
    return left_new[None], right_new[None]


def solution(mesh):
    return jax.shard_map(
        shards,
        mesh=mesh,
        in_specs=(
            P("bond", "sec", None, None),
            P("bond", "sec", None, None),
            P(),
            P(),
            P("bond", "sec"),
            P("bond", "sec", None, None),
        ),
        out_specs=(P("bond", "sec", None, None), P("bond", "sec", None, None)),
        check_vma=False,
    )
```

```python
import functools
import jax
import jax.numpy as jnp
from jax import lax
from jax.experimental import pallas as pl
from jax.experimental.pallas import tpu as pltpu
from jax.sharding import PartitionSpec as P

MESH = pl.DeviceIdType.MESH
ITERS=4
NB=16
F32=jnp.float32; BF=jnp.bfloat16

def split3(x):
    h=x.astype(BF)
    r=x-h.astype(F32)
    m=r.astype(BF)
    l=(r-m.astype(F32)).astype(BF)
    return h,m,l

def split2(x):
    h = x.astype(BF)
    return h, (x - h.astype(F32)).astype(BF)


def dot(a,b,ca,cb):
    return lax.dot_general(a,b,(((ca,),(cb,)),((),())),preferred_element_type=F32)

def factor(aug, ubuf, tri, n, nb, S):
    for t in range(n//nb):
        lo=t*nb
        X=[aug[pl.ds(lo+k,2*S,stride=n),:] for k in range(nb)]
        v={}
        for i in range(nb):
            xa=jnp.concatenate([X[i][:S],X[i][:S]],axis=0)
            for k in range(i+1):
                v[i,k]=jnp.broadcast_to(xa[:,lo+k:lo+k+1],(2*S,n))
        U=[None]*nb
        for j in range(nb):
            r=lax.rsqrt(v[j,j])
            U[j]=X[j]*r
            tri[pl.ds(lo+j,S,stride=n),:]=U[j][S:]
            ubuf[pl.ds(j,2*S,stride=nb),:]=U[j]
            col={}
            for i in range(j+1,nb):
                col[i]=v[i,j]*r
            for i in range(j+1,nb):
                for k in range(j+1,i+1):
                    v[i,k]=v[i,k]-col[i]*col[k]
                X[i]=X[i]-col[i]*U[j]
        if lo+nb<n:
            for s in range(S):
                h,m,l=split3(ubuf[s*nb:(s+1)*nb,:])
                lhs=jnp.concatenate([h,h,m,h,m,l],axis=0)
                rhs=jnp.concatenate([h,m,h,l,m,h],axis=0)
                h,m,l=split3(ubuf[(S+s)*nb:(S+s+1)*nb,:])
                rhs2=jnp.concatenate([h,m,h,l,m,h],axis=0)
                up=dot(lhs,jnp.concatenate([rhs,rhs2],axis=1),0,0)
                rows=slice(s*n+lo+nb,(s+1)*n)
                aug[rows,:]=aug[rows,:]-up[lo+nb:,:n]
                rows=slice((S+s)*n+lo+nb,(S+s+1)*n)
                aug[rows,:]=aug[rows,:]-up[lo+nb:,n:]


def sum_rows(x, n):
    total = x[:n]
    for i in range(1, x.shape[0] // n):
        total = total + x[i * n:(i + 1) * n]
    return total


def layer_body(left, right, gate, sign, kept, start, left_new, right_new,
               left_v, partner, pair, below, above, theta, gram, start_v, gate_v, sign_v,
               bt, gt, aug, ubuf, tri, out,
               lsem, rs_sem, rr_sem, ps_sem, pr_sem, os_sem, or_sem):
    S, d, _ = left_v.shape
    n = bt.shape[1]
    bond, bonds = lax.axis_index("bond"), lax.axis_size("bond")
    f, nf = lax.axis_index("sec"), lax.axis_size("sec")
    ahead, behind = lax.rem(bond + 1, bonds), lax.rem(bond + bonds - 1, bonds)
    has_lo, has_hi = f > 0, f < nf - 1

    def load(q):
        return pltpu.make_async_copy(left.at[q], left_v.at[q], lsem.at[q])

    small = [
        pltpu.make_async_copy(start, start_v, lsem.at[S]),
        pltpu.make_async_copy(gate, gate_v, lsem.at[S + 1]),
        pltpu.make_async_copy(sign, sign_v, lsem.at[S + 2]),
    ]

    def shift(q):
        return pltpu.make_async_remote_copy(
            src_ref=right.at[q], dst_ref=partner.at[q], send_sem=rs_sem.at[q],
            recv_sem=rr_sem.at[q], device_id={"bond": behind}, device_id_type=MESH)

    def up(q):
        return pltpu.make_async_remote_copy(
            src_ref=pair.at[q], dst_ref=below.at[q], send_sem=ps_sem.at[0, q],
            recv_sem=pr_sem.at[0, q], device_id={"sec": f + 1}, device_id_type=MESH)

    def down(q):
        return pltpu.make_async_remote_copy(
            src_ref=pair.at[q], dst_ref=above.at[q], send_sem=ps_sem.at[1, q],
            recv_sem=pr_sem.at[1, q], device_id={"sec": f - 1}, device_id_type=MESH)

    def back(s):
        return pltpu.make_async_remote_copy(
            src_ref=out.at[s], dst_ref=right_new.at[s], send_sem=os_sem.at[s],
            recv_sem=or_sem.at[s], device_id={"bond": ahead}, device_id_type=MESH)

    barrier = pltpu.get_barrier_semaphore()
    pl.semaphore_signal(barrier, inc=1, device_id={"bond": ahead}, device_id_type=MESH)
    pl.semaphore_signal(barrier, inc=1, device_id={"bond": behind}, device_id_type=MESH)

    @pl.when(has_lo)
    def _():
        pl.semaphore_signal(barrier, inc=1, device_id={"sec": f - 1}, device_id_type=MESH)

    @pl.when(has_hi)
    def _():
        pl.semaphore_signal(barrier, inc=1, device_id={"sec": f + 1}, device_id_type=MESH)

    for q in range(S):
        load(q).start()
    for copy in small:
        copy.start()
    pl.semaphore_wait(barrier, 2 + has_lo.astype(jnp.int32) + has_hi.astype(jnp.int32))
    for q in range(S):
        shift(q).start()

    @pl.when(jnp.logical_not(has_lo))
    def _():
        below[...] = jnp.zeros_like(below)

    @pl.when(jnp.logical_not(has_hi))
    def _():
        above[...] = jnp.zeros_like(above)

    def multiply(q, c):
        load(q).wait()
        shift(q).wait_recv()

        def rows(i, c):
            at = pl.ds(pl.multiple_of(i * 128, 128), 128)
            pair[q, at, :] = dot(left_v[q, at, :], partner[q], 1, 0).astype(BF)
            return c

        lax.fori_loop(0, d // 128, rows, 0)

        @pl.when(has_hi)
        def _():
            up(q).start()

        @pl.when(has_lo)
        def _():
            down(q).start()

        return c

    lax.fori_loop(0, S, multiply, 0)
    for copy in small:
        copy.wait()

    firsts = (jnp.maximum(f - 1, 0), f, jnp.minimum(f + 1, nf - 1))
    here = (has_lo.astype(F32), None, has_hi.astype(F32))

    def arrive(q):
        @pl.when(has_lo)
        def _():
            up(q).wait_recv()

        @pl.when(has_hi)
        def _():
            down(q).wait_recv()

    def mix(p):
        terms = []
        for first, gone, block in zip(firsts, here, (below, pair, above)):
            for q in range(max(0, p - 1), min(S, p + 2)):
                row, column = f * S + p, first * S + q
                w = gate_v[row, column] * (1.0 - 2.0 * sign_v[row, column].astype(F32))
                terms.append((w if gone is None else w * gone, block, q))

        def rows(i, c):
            at = pl.ds(pl.multiple_of(i * 16, 16), 16)
            total = None
            for w, block, q in terms:
                term = w * block[q, at, :].astype(F32)
                total = term if total is None else total + term
            theta[p, at, :] = total.astype(BF)
            return c

        lax.fori_loop(0, d // 16, rows, 0)

    def grow(s, b):
        h, m = split2(b)
        g = (sum_rows(dot(jnp.concatenate([h, m], axis=0), gram[s, 0], 1, 0), n)
             + dot(h, gram[s, 1], 1, 0))
        gt[s] = g
        hm = jnp.concatenate(split2(g), axis=0)
        o = dot(hm, hm, 1, 1)
        aug[pl.ds(pl.multiple_of(s * n, n), n), :] = (o[:n, :n] + o[n:, n:]) + (o[:n, n:] + o[n:, :n])
        eye = (lax.broadcasted_iota(jnp.int32, (n, n), 0)
               == lax.broadcasted_iota(jnp.int32, (n, n), 1)).astype(F32)
        aug[pl.ds(pl.multiple_of((S + s) * n, n), n), :] = eye

    def begin(s, c):
        def rows(i, c):
            at = pl.ds(pl.multiple_of(i * 128, 128), 128)
            h, m = split2(dot(theta[s, at, :], theta[s], 1, 1))
            gram[s, 0, at, :] = h
            gram[s, 1, at, :] = m
            return c

        lax.fori_loop(0, d // 128, rows, 0)
        grow(s, start_v[s].T)
        return c

    arrive(0)
    arrive(1)
    mix(0)
    arrive(2)
    mix(1)
    arrive(3)
    mix(2)
    mix(3)
    lax.fori_loop(0, S, begin, 0)

    def step(it, c):
        factor(aug, ubuf, tri, n, NB, S)

        def normal(s, c):
            a, b, l = split3(tri[pl.ds(pl.multiple_of(s * n, n), n), :])
            lhs = jnp.concatenate([jnp.concatenate([x, x], axis=1) for x in (a, b, l)], axis=0)
            basis = sum_rows(dot(lhs, jnp.concatenate(split2(gt[s]), axis=0), 1, 0), n)

            @pl.when(it < ITERS - 1)
            def _():
                grow(s, basis)

            @pl.when(it == ITERS - 1)
            def _():
                bt[s] = basis

            return c

        lax.fori_loop(0, S, normal, 0)
        return c

    lax.fori_loop(0, ITERS, step, 0)
    row = lax.broadcasted_iota(jnp.int32, (n, d), 0)
    for s in range(S):
        masked = jnp.where(row < kept[0, s], bt[s], 0.0)
        out[s] = sum_rows(dot(jnp.concatenate(split2(masked), axis=0), theta[s], 1, 0), n).astype(BF)
        back(s).start()
    for s in range(S):
        left_new[s] = jnp.where(row < kept[0, s], bt[s], 0.0).T.astype(BF)
    for q in range(S):
        shift(q).wait_send()

        @pl.when(has_hi)
        def _():
            up(q).wait_send()

        @pl.when(has_lo)
        def _():
            down(q).wait_send()

    for s in range(S):
        back(s).wait()


def layer(left, right, gate, sign, kept, start):
    S, d, n = start.shape
    block = pltpu.VMEM((S, d, d), BF)
    dma = pltpu.SemaphoreType.DMA
    hbm = pl.BlockSpec(memory_space=pl.ANY)
    smem = pl.BlockSpec(memory_space=pltpu.SMEM)
    return pl.pallas_call(
        layer_body,
        out_shape=(jax.ShapeDtypeStruct((S, d, n), BF), jax.ShapeDtypeStruct((S, n, d), BF)),
        in_specs=[hbm, hbm, hbm, hbm, smem, hbm],
        out_specs=[pl.BlockSpec(memory_space=pltpu.VMEM), hbm],
        scratch_shapes=[block] * 6 + [
            pltpu.VMEM((S, 2, d, d), BF),
            pltpu.VMEM((S, d, n), F32),
            pltpu.SMEM(gate.shape, F32),
            pltpu.SMEM(sign.shape, jnp.int32),
            pltpu.VMEM((S, n, d), F32),
            pltpu.VMEM((S, n, d), F32),
            pltpu.VMEM((2 * S * n, n), F32),
            pltpu.VMEM((2 * S * NB, n), F32),
            pltpu.VMEM((S * n, n), F32),
            pltpu.VMEM((S, n, d), BF),
            dma((S + 3,)), dma((S,)), dma((S,)), dma((2, S)), dma((2, S)), dma((S,)), dma((S,)),
        ],
        compiler_params=pltpu.CompilerParams(
            collective_id=0, has_side_effects=True, vmem_limit_bytes=56 * 2**20),
    )(left, right, gate, sign, kept, start)


def shards(left_site, right_site, gate, sign_table, kept, start):
    left_new, right_new = layer(left_site[0], right_site[0], gate, sign_table, kept, start[0])
    return left_new[None], right_new[None]


def solution(mesh):
    return jax.shard_map(
        shards,
        mesh=mesh,
        in_specs=(
            P("bond", "sec", None, None),
            P("bond", "sec", None, None),
            P(),
            P(),
            P("bond", "sec"),
            P("bond", "sec", None, None),
        ),
        out_specs=(P("bond", "sec", None, None), P("bond", "sec", None, None)),
        check_vma=False,
    )
```

```python
import functools
import jax
import jax.numpy as jnp
from jax import lax
from jax.experimental import pallas as pl
from jax.experimental.pallas import tpu as pltpu
from jax.sharding import PartitionSpec as P

MESH = pl.DeviceIdType.MESH
ITERS=4
NB=16
F32=jnp.float32; BF=jnp.bfloat16

def split3(x):
    h=x.astype(BF)
    r=x-h.astype(F32)
    m=r.astype(BF)
    l=(r-m.astype(F32)).astype(BF)
    return h,m,l

def split2(x):
    h = x.astype(BF)
    return h, (x - h.astype(F32)).astype(BF)


def dot(a,b,ca,cb):
    return lax.dot_general(a,b,(((ca,),(cb,)),((),())),preferred_element_type=F32)

def factor(aug, ubuf, nbuf, tri, n, S, nb, hook):
    lane=lax.broadcasted_iota(jnp.int32,(S,n),1)
    lane1=lax.broadcasted_iota(jnp.int32,(1,n),1)
    def bc(x,i): return jnp.broadcast_to(x[:,i:i+1],(S,n))
    def within(a,b): return jnp.logical_and(lane>=a,lane<b)
    X=[aug[pl.ds(k,S,stride=n),:] for k in range(nb)]
    for t in range(n//nb):
        lo=t*nb; end=lo+nb
        v={(i,k):bc(X[i],lo+k) for k in range(nb) for i in range(k,nb)}
        for j in range(nb):
            r=lax.rsqrt(v[j,j])
            U=jnp.where(lane==lo+j,r,X[j]*r)
            tri[pl.ds(lo+j,S,stride=n),:]=jnp.where(lane<=lo+j,U,0.0)
            if end<n:
                ubuf[pl.ds(j,S,stride=nb),:]=jnp.where(within(lo+j+1,end),0.0,U) if j<nb-1 else U
            col={i:v[i,j]*r for i in range(j+1,nb)}
            for i in range(j+1,nb):
                for k in range(j+1,i+1):
                    v[i,k]=v[i,k]-col[i]*col[k]
                X[i]=jnp.where(lane==lo+j,0.0,X[i])-col[i]*U
        if end<n:
            blk=jnp.logical_and(lane1>=lo,lane1<end)
            lt,rh=[],[]
            for s in range(S):
                h,m,l=split3(ubuf[s*nb:(s+1)*nb,:])
                lt.append(jnp.concatenate([h,h,m,h,m,l],axis=0).T)
                rh.append(jnp.concatenate([h,m,h,l,m,h],axis=0))
            o=dot(jnp.concatenate([x[end:end+nb] for x in lt],axis=0),jnp.concatenate(rh,axis=1),1,0)
            for s in range(S):
                nbuf[s*nb:(s+1)*nb,:]=jnp.where(blk,0.0,aug[s*n+end:s*n+end+nb,:])-o[s*nb:(s+1)*nb,s*n:(s+1)*n]
            X=[nbuf[pl.ds(k,S,stride=nb),:] for k in range(nb)]
            first=end+nb
            hook(t)
            if first<n:
                for s in range(S):
                    rows=slice(s*n+first,(s+1)*n)
                    aug[rows,:]=jnp.where(blk,0.0,aug[rows,:])-dot(lt[s][first:],rh[s],1,0)

def sum_rows(x, n):
    total = x[:n]
    for i in range(1, x.shape[0] // n):
        total = total + x[i * n:(i + 1) * n]
    return total


def layer_body(left, right, gate, sign, kept, start, left_new, right_new,
               left_v, partner, pair, below, above, theta, gram, start_v, gate_v, sign_v,
               bt, gt, ht, aug, ubuf, nbuf, tri, out,
               lsem, rs_sem, rr_sem, ps_sem, pr_sem, os_sem, or_sem, turn):
    S, d, _ = left_v.shape
    n = bt.shape[1]
    bond, bonds = lax.axis_index("bond"), lax.axis_size("bond")
    f, nf = lax.axis_index("sec"), lax.axis_size("sec")
    ahead, behind = lax.rem(bond + 1, bonds), lax.rem(bond + bonds - 1, bonds)
    has_lo, has_hi = f > 0, f < nf - 1
    even = lax.rem(bond, 2) == 0

    def load(q):
        return pltpu.make_async_copy(left.at[q], left_v.at[q], lsem.at[q])

    small = [
        pltpu.make_async_copy(start, start_v, lsem.at[S]),
        pltpu.make_async_copy(gate, gate_v, lsem.at[S + 1]),
        pltpu.make_async_copy(sign, sign_v, lsem.at[S + 2]),
    ]

    def shift(q):
        return pltpu.make_async_remote_copy(
            src_ref=right.at[q], dst_ref=partner.at[q], send_sem=rs_sem.at[q],
            recv_sem=rr_sem.at[q], device_id={"bond": behind}, device_id_type=MESH)

    def up(q):
        return pltpu.make_async_remote_copy(
            src_ref=pair.at[q], dst_ref=below.at[q], send_sem=ps_sem.at[0, q],
            recv_sem=pr_sem.at[0, q], device_id={"sec": f + 1}, device_id_type=MESH)

    def down(q):
        return pltpu.make_async_remote_copy(
            src_ref=pair.at[q], dst_ref=above.at[q], send_sem=ps_sem.at[1, q],
            recv_sem=pr_sem.at[1, q], device_id={"sec": f - 1}, device_id_type=MESH)

    def back(s):
        return pltpu.make_async_remote_copy(
            src_ref=out.at[s], dst_ref=right_new.at[s], send_sem=os_sem.at[s],
            recv_sem=or_sem.at[s], device_id={"bond": ahead}, device_id_type=MESH)

    barrier = pltpu.get_barrier_semaphore()
    pl.semaphore_signal(barrier, inc=1, device_id={"bond": ahead}, device_id_type=MESH)
    pl.semaphore_signal(barrier, inc=1, device_id={"bond": behind}, device_id_type=MESH)

    @pl.when(has_lo)
    def _():
        pl.semaphore_signal(barrier, inc=1, device_id={"sec": f - 1}, device_id_type=MESH)

    @pl.when(has_hi)
    def _():
        pl.semaphore_signal(barrier, inc=1, device_id={"sec": f + 1}, device_id_type=MESH)

    for q in range(S):
        load(q).start()
    for copy in small:
        copy.start()
    pl.semaphore_wait(barrier, 2 + has_lo.astype(jnp.int32) + has_hi.astype(jnp.int32))
    for q in range(S):
        shift(q).start()

    @pl.when(jnp.logical_not(has_lo))
    def _():
        below[...] = jnp.zeros_like(below)

    @pl.when(jnp.logical_not(has_hi))
    def _():
        above[...] = jnp.zeros_like(above)

    def multiply(q, c):
        load(q).wait()
        shift(q).wait_recv()

        def rows(i, c):
            at = pl.ds(pl.multiple_of(i * 128, 128), 128)
            pair[q, at, :] = dot(left_v[q, at, :], partner[q], 1, 0).astype(BF)
            return c

        lax.fori_loop(0, d // 128, rows, 0)

        @pl.when(jnp.logical_and(even, q == S - 1))
        def _():
            pl.semaphore_wait(turn, 1)

        @pl.when(has_hi)
        def _():
            up(q).start()

        @pl.when(has_lo)
        def _():
            down(q).start()

        return c

    lax.fori_loop(0, S, multiply, 0)
    for copy in small:
        copy.wait()
    for s in range(S):
        bt[s] = start_v[s].T

    @pl.when(jnp.logical_not(even))
    def _():
        for q in range(S):
            @pl.when(has_hi)
            def _():
                up(q).wait_send()

            @pl.when(has_lo)
            def _():
                down(q).wait_send()

        pl.semaphore_signal(turn, inc=1, device_id={"bond": behind}, device_id_type=MESH)


    firsts = (jnp.maximum(f - 1, 0), f, jnp.minimum(f + 1, nf - 1))
    here = (has_lo.astype(F32), None, has_hi.astype(F32))

    def arrive(q):
        @pl.when(has_lo)
        def _():
            up(q).wait_recv()

        @pl.when(has_hi)
        def _():
            down(q).wait_recv()

    def mix(p):
        terms = []
        for first, gone, block in zip(firsts, here, (below, pair, above)):
            for q in range(max(0, p - 1), min(S, p + 2)):
                row, column = f * S + p, first * S + q
                w = gate_v[row, column] * (1.0 - 2.0 * sign_v[row, column].astype(F32))
                terms.append((w if gone is None else w * gone, block, q))

        def rows(i, c):
            at = pl.ds(pl.multiple_of(i * 16, 16), 16)
            total = None
            for w, block, q in terms:
                term = w * block[q, at, :].astype(F32)
                total = term if total is None else total + term
            theta[p, at, :] = total.astype(BF)
            return c

        lax.fori_loop(0, d // 16, rows, 0)

    def by_gram(s, x):
        h, m = split2(x)
        return (sum_rows(dot(jnp.concatenate([h, m], axis=0), gram[s, 0], 1, 0), n)
                + dot(h, gram[s, 1], 1, 0))

    def by_tri(s, x):
        a, b, l = split3(tri[s * n:(s + 1) * n, :])
        lhs = jnp.concatenate([jnp.concatenate([y, y], axis=1) for y in (a, b, l)], axis=0)
        return sum_rows(dot(lhs, jnp.concatenate(split2(x), axis=0), 1, 0), n)

    def put(s, g):
        gt[s] = g
        hm = jnp.concatenate(split2(g), axis=0)
        o = dot(hm, hm, 1, 1)
        aug[s * n:(s + 1) * n, :] = (o[:n, :n] + o[n:, n:]) + (o[:n, n:] + o[n:, :n])

    def begin(s):
        def rows(i, c):
            at = pl.ds(pl.multiple_of(i * 128, 128), 128)
            h, m = split2(dot(theta[s, at, :], theta[s], 1, 1))
            gram[s, 0, at, :] = h
            gram[s, 1, at, :] = m
            return c

        lax.fori_loop(0, d // 128, rows, 0)
        put(s, by_gram(s, bt[s]))

    arrive(0)
    arrive(1)
    mix(0)
    begin(0)
    arrive(2)
    mix(1)
    begin(1)
    arrive(3)
    mix(2)
    mix(3)
    begin(2)
    begin(3)

    def step(it, c):
        def meanwhile(t):
            if t % 2 == 0 and t // 2 < S:
                ht[t // 2] = by_gram(t // 2, gt[t // 2])

        factor(aug, ubuf, nbuf, tri, n, S, NB, meanwhile)

        @pl.when(it < ITERS - 1)
        def _():
            for s in range(S):
                put(s, by_tri(s, ht[s]))

        return c

    lax.fori_loop(0, ITERS, step, 0)
    row = lax.broadcasted_iota(jnp.int32, (n, d), 0)
    for s in range(S):
        masked = jnp.where(row < kept[0, s], by_tri(s, gt[s]), 0.0)
        bt[s] = masked
        out[s] = sum_rows(dot(jnp.concatenate(split2(masked), axis=0), theta[s], 1, 0), n).astype(BF)
        back(s).start()
    for s in range(S):
        left_new[s] = bt[s].T.astype(BF)
    for q in range(S):
        shift(q).wait_send()

        @pl.when(jnp.logical_and(even, has_hi))
        def _():
            up(q).wait_send()

        @pl.when(jnp.logical_and(even, has_lo))
        def _():
            down(q).wait_send()

    for s in range(S):
        back(s).wait()


def layer(left, right, gate, sign, kept, start):
    S, d, n = start.shape
    block = pltpu.VMEM((S, d, d), BF)
    dma = pltpu.SemaphoreType.DMA
    hbm = pl.BlockSpec(memory_space=pltpu.HBM)
    smem = pl.BlockSpec(memory_space=pltpu.SMEM)
    return pl.pallas_call(
        layer_body,
        out_shape=(jax.ShapeDtypeStruct((S, d, n), BF), jax.ShapeDtypeStruct((S, n, d), BF)),
        in_specs=[hbm, hbm, hbm, hbm, smem, hbm],
        out_specs=[pl.BlockSpec(memory_space=pltpu.VMEM), pl.BlockSpec(memory_space=pl.ANY)],
        scratch_shapes=[block] * 6 + [
            pltpu.VMEM((S, 2, d, d), BF),
            pltpu.VMEM((S, d, n), F32),
            pltpu.SMEM(gate.shape, F32),
            pltpu.SMEM(sign.shape, jnp.int32),
            pltpu.VMEM((S, n, d), F32),
            pltpu.VMEM((S, n, d), F32),
            pltpu.VMEM((S, n, d), F32),
            pltpu.VMEM((S * n, n), F32),
            pltpu.VMEM((S * NB, n), F32),
            pltpu.VMEM((S * NB, n), F32),
            pltpu.VMEM((S * n, n), F32),
            pltpu.VMEM((S, n, d), BF),
            dma((S + 3,)), dma((S,)), dma((S,)), dma((2, S)), dma((2, S)), dma((S,)), dma((S,)),
            pltpu.SemaphoreType.REGULAR,
        ],
        compiler_params=pltpu.CompilerParams(
            collective_id=0, has_side_effects=True, vmem_limit_bytes=52 * 2**20),
    )(left, right, gate, sign, kept, start)


def shards(left_site, right_site, gate, sign_table, kept, start):
    left_new, right_new = layer(left_site[0], right_site[0], gate, sign_table, kept, start[0])
    return left_new[None], right_new[None]


def solution(mesh):
    return jax.shard_map(
        shards,
        mesh=mesh,
        in_specs=(
            P("bond", "sec", None, None),
            P("bond", "sec", None, None),
            P(),
            P(),
            P("bond", "sec"),
            P("bond", "sec", None, None),
        ),
        out_specs=(P("bond", "sec", None, None), P("bond", "sec", None, None)),
        check_vma=False,
    )
```

```python
import functools
import jax
import jax.numpy as jnp
from jax import lax
from jax.experimental import pallas as pl
from jax.experimental.pallas import tpu as pltpu
from jax.sharding import PartitionSpec as P

MESH = pl.DeviceIdType.MESH
ITERS = 4
NB = 16
F32=jnp.float32; BF=jnp.bfloat16

def split3(x):
    h=x.astype(BF)
    r=x-h.astype(F32)
    m=r.astype(BF)
    l=(r-m.astype(F32)).astype(BF)
    return h,m,l

def split2(x):
    h = x.astype(BF)
    return h, (x - h.astype(F32)).astype(BF)


def dot(a,b,ca,cb):
    return lax.dot_general(a,b,(((ca,),(cb,)),((),())),preferred_element_type=F32)

def factor(aug, ubuf, nbuf, tri, n, S, nb, hook):
    lane=lax.broadcasted_iota(jnp.int32,(S,n),1)
    lane1=lax.broadcasted_iota(jnp.int32,(1,n),1)
    def bc(x,i): return jnp.broadcast_to(x[:,i:i+1],(S,n))
    def within(a,b): return jnp.logical_and(lane>=a,lane<b)
    X=[aug[pl.ds(k,S,stride=n),:] for k in range(nb)]
    for t in range(n//nb):
        lo=t*nb; end=lo+nb
        v={(i,k):bc(X[i],lo+k) for k in range(nb) for i in range(k,nb)}
        for j in range(nb):
            r=lax.rsqrt(v[j,j])
            U=jnp.where(lane==lo+j,r,X[j]*r)
            tri[pl.ds(lo+j,S,stride=n),:]=jnp.where(lane<=lo+j,U,0.0)
            if end<n:
                ubuf[pl.ds(j,S,stride=nb),:]=jnp.where(within(lo+j+1,end),0.0,U) if j<nb-1 else U
            col={i:v[i,j]*r for i in range(j+1,nb)}
            for i in range(j+1,nb):
                for k in range(j+1,i+1):
                    v[i,k]=v[i,k]-col[i]*col[k]
                X[i]=jnp.where(lane==lo+j,0.0,X[i])-col[i]*U
        if end<n:
            blk=jnp.logical_and(lane1>=lo,lane1<end)
            lt,rh=[],[]
            for s in range(S):
                h,m,l=split3(ubuf[s*nb:(s+1)*nb,:])
                lt.append(jnp.concatenate([h,h,m,h,m,l],axis=0).T)
                rh.append(jnp.concatenate([h,m,h,l,m,h],axis=0))
            o=dot(jnp.concatenate([x[end:end+nb] for x in lt],axis=0),jnp.concatenate(rh,axis=1),1,0)
            for s in range(S):
                nbuf[s*nb:(s+1)*nb,:]=jnp.where(blk,0.0,aug[s*n+end:s*n+end+nb,:])-o[s*nb:(s+1)*nb,s*n:(s+1)*n]
            X=[nbuf[pl.ds(k,S,stride=nb),:] for k in range(nb)]
            first=end+nb
            hook(t)
            if first<n:
                for s in range(S):
                    rows=slice(s*n+first,(s+1)*n)
                    aug[rows,:]=jnp.where(blk,0.0,aug[rows,:])-dot(lt[s][first:],rh[s],1,0)

def sum_rows(x, n):
    total = x[:n]
    for i in range(1, x.shape[0] // n):
        total = total + x[i * n:(i + 1) * n]
    return total


def layer_body(left, right, table, start, left_new, right_new,
               left_v, partner, pair, below, above, theta, total, gram, start_v, table_v,
               bt, gt, ht, aug, ubuf, nbuf, tri, out,
               lsem, rs_sem, rr_sem, ps_sem, pr_sem, os_sem, or_sem, turn):
    S, d, _ = left_v.shape
    n = bt.shape[1]
    bond, bonds = lax.axis_index("bond"), lax.axis_size("bond")
    f, nf = lax.axis_index("sec"), lax.axis_size("sec")
    ahead, behind = lax.rem(bond + 1, bonds), lax.rem(bond + bonds - 1, bonds)
    has_lo, has_hi = f > 0, f < nf - 1
    odd = lax.rem(bond, 2) == 1

    half = d // 2

    def cols(h):
        return pl.ds(pl.multiple_of(h * half, half), half)

    def load(q):
        return pltpu.make_async_copy(left.at[q], left_v.at[q], lsem.at[q])

    small = [
        pltpu.make_async_copy(start, start_v, lsem.at[S]),
        pltpu.make_async_copy(table, table_v, lsem.at[S + 1]),
    ]

    def shift(q, h):
        return pltpu.make_async_remote_copy(
            src_ref=right.at[q, :, cols(h)], dst_ref=partner.at[q, :, cols(h)],
            send_sem=rs_sem.at[q, h], recv_sem=rr_sem.at[q, h],
            device_id={"bond": behind}, device_id_type=MESH)

    def up(q, h):
        return pltpu.make_async_remote_copy(
            src_ref=pair.at[q, :, cols(h)], dst_ref=below.at[q, :, cols(h)],
            send_sem=ps_sem.at[0, q, h], recv_sem=pr_sem.at[0, q, h],
            device_id={"sec": f + 1}, device_id_type=MESH)

    def down(q, h):
        return pltpu.make_async_remote_copy(
            src_ref=pair.at[q, :, cols(h)], dst_ref=above.at[q, :, cols(h)],
            send_sem=ps_sem.at[1, q, h], recv_sem=pr_sem.at[1, q, h],
            device_id={"sec": f - 1}, device_id_type=MESH)

    def back(s):
        return pltpu.make_async_remote_copy(
            src_ref=out.at[s], dst_ref=right_new.at[s], send_sem=os_sem.at[s],
            recv_sem=or_sem.at[s], device_id={"bond": ahead}, device_id_type=MESH)

    def both(act, where=True):
        @pl.when(jnp.logical_and(where, has_hi))
        def _():
            act(up)

        @pl.when(jnp.logical_and(where, has_lo))
        def _():
            act(down)

    barrier = pltpu.get_barrier_semaphore()
    pl.semaphore_signal(barrier, inc=1, device_id={"bond": ahead}, device_id_type=MESH)
    pl.semaphore_signal(barrier, inc=1, device_id={"bond": behind}, device_id_type=MESH)

    @pl.when(has_lo)
    def _():
        pl.semaphore_signal(barrier, inc=1, device_id={"sec": f - 1}, device_id_type=MESH)

    @pl.when(has_hi)
    def _():
        pl.semaphore_signal(barrier, inc=1, device_id={"sec": f + 1}, device_id_type=MESH)

    for q in range(S):
        load(q).start()
    for copy in small:
        copy.start()
    pl.semaphore_wait(barrier, 2 + has_lo.astype(jnp.int32) + has_hi.astype(jnp.int32))
    for q in range(S):
        for h in range(2):
            shift(q, h).start()

    def multiply(i, c):
        q, h = i // 2, lax.rem(i, 2)

        @pl.when(h == 0)
        def _():
            load(q).wait()

        shift(q, h).wait_recv()
        pair[q, :, cols(h)] = dot(left_v[q], partner[q, :, cols(h)], 1, 0).astype(BF)
        both(lambda way: way(q, h).start(), jnp.logical_or(odd, q < S - 1))
        return c

    lax.fori_loop(0, 2 * S, multiply, 0)

    @pl.when(jnp.logical_not(has_lo))
    def _():
        below[...] = jnp.zeros_like(below)

    @pl.when(jnp.logical_not(has_hi))
    def _():
        above[...] = jnp.zeros_like(above)

    for copy in small:
        copy.wait()
    for s in range(S):
        bt[s] = start_v[s].T

    firsts = (jnp.maximum(f - 1, 0), f, jnp.minimum(f + 1, nf - 1))
    here = (has_lo.astype(F32), None, has_hi.astype(F32))

    def arrive(q, h):
        @pl.when(has_lo)
        def _():
            up(q, h).wait_recv()

        @pl.when(has_hi)
        def _():
            down(q, h).wait_recv()

    def mix(p, h):
        terms = []
        for first, gone, block in zip(firsts, here, (below, pair, above)):
            for q in range(max(0, p - 1), min(S, p + 2)):
                w = table_v[f * S + p, first * S + q]
                terms.append((w if gone is None else w * gone, block, q))

        def rows(i, c):
            at = pl.ds(pl.multiple_of(i * 32, 32), 32)
            total = None
            for w, block, q in terms:
                term = w * block[q, at, h * half:(h + 1) * half].astype(F32)
                total = term if total is None else total + term
            theta[p, at, h * half:(h + 1) * half] = total.astype(BF)
            return c

        lax.fori_loop(0, d // 32, rows, 0)

    def square(s, h):
        for k in range(2):
            part = slice(k * half, (k + 1) * half)
            wide = slice(h * half, (h + 1) * half)
            o = dot(theta[s, :, wide], theta[s, part, wide], 1, 1)
            if h == 0:
                total[s % 2, :, part] = o
            else:
                hi, lo = split2(total[s % 2, :, part] + o)
                gram[s, 0, :, part] = hi
                gram[s, 1, :, part] = lo

    def by_gram(s, x):
        h, m = split2(x)
        return (sum_rows(dot(jnp.concatenate([h, m], axis=0), gram[s, 0], 1, 0), n)
                + dot(h, gram[s, 1], 1, 0))

    def by_tri(s, x):
        a, b, l = split3(tri[s * n:(s + 1) * n, :])
        lhs = jnp.concatenate([jnp.concatenate([y, y], axis=1) for y in (a, b, l)], axis=0)
        return sum_rows(dot(lhs, jnp.concatenate(split2(x), axis=0), 1, 0), n)

    def put(s, g):
        gt[s] = g
        hm = jnp.concatenate(split2(g), axis=0)
        o = dot(hm, hm, 1, 1)
        aug[s * n:(s + 1) * n, :] = (o[:n, :n] + o[n:, n:]) + (o[:n, n:] + o[n:, :n])

    def begin(s):
        for h in range(2):
            mix(s, h)
            square(s, h)
        put(s, by_gram(s, bt[s]))

    for q in range(2):
        for h in range(2):
            arrive(q, h)
    begin(0)

    @pl.when(odd)
    def _():
        for q in range(S):
            for h in range(2):
                both(lambda way: way(q, h).wait_send())
        pl.semaphore_signal(turn, inc=1, device_id={"bond": behind}, device_id_type=MESH)

    @pl.when(jnp.logical_not(odd))
    def _():
        pl.semaphore_wait(turn, 1)
        for h in range(2):
            both(lambda way: way(S - 1, h).start())

    for h in range(2):
        arrive(2, h)
    begin(1)
    for h in range(2):
        arrive(3, h)
        for s in (2, 3):
            mix(s, h)
            square(s, h)
    for s in (2, 3):
        put(s, by_gram(s, bt[s]))

    def step(it, c):
        def meanwhile(t):
            if t % 2 == 0 and t // 2 < S:
                ht[t // 2] = by_gram(t // 2, gt[t // 2])

        factor(aug, ubuf, nbuf, tri, n, S, NB, meanwhile)

        @pl.when(it < ITERS - 1)
        def _():
            for s in range(S):
                put(s, by_tri(s, ht[s]))

        return c

    lax.fori_loop(0, ITERS, step, 0)
    row = lax.broadcasted_iota(jnp.int32, (n, d), 0).astype(F32)
    for s in range(S):
        masked = jnp.where(row < table_v[nf * S, s], by_tri(s, gt[s]), 0.0)
        bt[s] = masked
        out[s] = sum_rows(dot(jnp.concatenate(split2(masked), axis=0), theta[s], 1, 0), n).astype(BF)
        back(s).start()
    for s in range(S):
        left_new[s] = bt[s].T.astype(BF)
    for q in range(S):
        for h in range(2):
            shift(q, h).wait_send()
            both(lambda way: way(q, h).wait_send(), jnp.logical_not(odd))

    for s in range(S):
        back(s).wait()


def layer(left, right, table, start):
    S, d, n = start.shape
    block = pltpu.VMEM((S, d, d), BF)
    dma = pltpu.SemaphoreType.DMA
    hbm = pl.BlockSpec(memory_space=pltpu.HBM)
    return pl.pallas_call(
        layer_body,
        out_shape=(jax.ShapeDtypeStruct((S, d, n), BF), jax.ShapeDtypeStruct((S, n, d), BF)),
        in_specs=[hbm] * 4,
        out_specs=[pl.BlockSpec(memory_space=pltpu.VMEM), pl.BlockSpec(memory_space=pl.ANY)],
        scratch_shapes=[block] * 6 + [
            pltpu.VMEM((2, d, d), F32),
            pltpu.VMEM((S, 2, d, d), BF),
            pltpu.VMEM((S, d, n), F32),
            pltpu.SMEM(table.shape, F32),
            pltpu.VMEM((S, n, d), F32),
            pltpu.VMEM((S, n, d), F32),
            pltpu.VMEM((S, n, d), F32),
            pltpu.VMEM((S * n, n), F32),
            pltpu.VMEM((S * NB, n), F32),
            pltpu.VMEM((S * NB, n), F32),
            pltpu.VMEM((S * n, n), F32),
            pltpu.VMEM((S, n, d), BF),
            dma((S + 2,)), dma((S, 2)), dma((S, 2)), dma((2, S, 2)), dma((2, S, 2)), dma((S,)), dma((S,)),
            pltpu.SemaphoreType.REGULAR,
        ],
        compiler_params=pltpu.CompilerParams(
            collective_id=0, has_side_effects=True, vmem_limit_bytes=52 * 2**20),
    )(left, right, table, start)


def shards(left_site, right_site, gate, sign_table, kept, start):
    coef = gate * (1.0 - 2.0 * sign_table.astype(F32))
    counts = jnp.pad(kept.astype(F32), ((0, 0), (0, gate.shape[1] - kept.shape[1])))
    table = jnp.concatenate([coef, counts], axis=0)
    left_new, right_new = layer(left_site[0], right_site[0], table, start[0])
    return left_new[None], right_new[None]


def solution(mesh):
    return jax.shard_map(
        shards,
        mesh=mesh,
        in_specs=(
            P("bond", "sec", None, None),
            P("bond", "sec", None, None),
            P(),
            P(),
            P("bond", "sec"),
            P("bond", "sec", None, None),
        ),
        out_specs=(P("bond", "sec", None, None), P("bond", "sec", None, None)),
        check_vma=False,
    )
```

```python
import functools
import jax
import jax.numpy as jnp
from jax import lax
from jax.experimental import pallas as pl
from jax.experimental.pallas import tpu as pltpu
from jax.sharding import PartitionSpec as P

MESH = pl.DeviceIdType.MESH
ITERS = 4
NB = 16
F32=jnp.float32; BF=jnp.bfloat16

def split3(x):
    h=x.astype(BF)
    r=x-h.astype(F32)
    m=r.astype(BF)
    l=(r-m.astype(F32)).astype(BF)
    return h,m,l

def split2(x):
    h = x.astype(BF)
    return h, (x - h.astype(F32)).astype(BF)


def dot(a,b,ca,cb):
    return lax.dot_general(a,b,(((ca,),(cb,)),((),())),preferred_element_type=F32)

def factor(aug, ubuf, nbuf, tri, n, S, nb, hook):
    lane=lax.broadcasted_iota(jnp.int32,(S,n),1)
    lane1=lax.broadcasted_iota(jnp.int32,(1,n),1)
    def bc(x,i): return jnp.broadcast_to(x[:,i:i+1],(S,n))
    def within(a,b): return jnp.logical_and(lane>=a,lane<b)
    X=[aug[pl.ds(k,S,stride=n),:] for k in range(nb)]
    for t in range(n//nb):
        lo=t*nb; end=lo+nb
        v={(i,k):bc(X[i],lo+k) for k in range(nb) for i in range(k,nb)}
        X=[jnp.where(within(lo,end),0.0,x) for x in X]
        for j in range(nb):
            r=lax.rsqrt(v[j,j])
            U=jnp.where(lane==lo+j,r,X[j]*r)
            tri[pl.ds(lo+j,S,stride=n),:]=jnp.where(lane<=lo+j,U,0.0)
            if end<n:
                ubuf[pl.ds(j,S,stride=nb),:]=U
            col={i:v[i,j]*r for i in range(j+1,nb)}
            for i in range(j+1,nb):
                for k in range(j+1,i+1):
                    v[i,k]=v[i,k]-col[i]*col[k]
                X[i]=X[i]-col[i]*U
        if end<n:
            blk=jnp.logical_and(lane1>=lo,lane1<end)
            lt,rh=[],[]
            for s in range(S):
                h,m,l=split3(ubuf[s*nb:(s+1)*nb,:])
                lt.append(jnp.concatenate([h,h,m,h,m,l],axis=0).T)
                rh.append(jnp.concatenate([h,m,h,l,m,h],axis=0))
            o=dot(jnp.concatenate([x[end:end+nb] for x in lt],axis=0),jnp.concatenate(rh,axis=1),1,0)
            for s in range(S):
                nbuf[s*nb:(s+1)*nb,:]=jnp.where(blk,0.0,aug[s*n+end:s*n+end+nb,:])-o[s*nb:(s+1)*nb,s*n:(s+1)*n]
            X=[nbuf[pl.ds(k,S,stride=nb),:] for k in range(nb)]
            first=end+nb
            hook(t)
            if first<n:
                for s in range(S):
                    rows=slice(s*n+first,(s+1)*n)
                    aug[rows,:]=jnp.where(blk,0.0,aug[rows,:])-dot(lt[s][first:],rh[s],1,0)

def sum_rows(x, n):
    total = x[:n]
    for i in range(1, x.shape[0] // n):
        total = total + x[i * n:(i + 1) * n]
    return total


def layer_body(left, right, table, start, left_new, right_new,
               left_v, partner, pair, below, above, theta, total, gram, start_v, table_v,
               bt, gt, ht, aug, ubuf, nbuf, tri, out,
               lsem, rs_sem, rr_sem, ps_sem, pr_sem, os_sem, or_sem, turn):
    S, d, _ = left_v.shape
    n = bt.shape[1]
    bond, bonds = lax.axis_index("bond"), lax.axis_size("bond")
    f, nf = lax.axis_index("sec"), lax.axis_size("sec")
    ahead, behind = lax.rem(bond + 1, bonds), lax.rem(bond + bonds - 1, bonds)
    has_lo, has_hi = f > 0, f < nf - 1
    odd = lax.rem(bond, 2) == 1

    half = d // 2

    def cols(h):
        return pl.ds(pl.multiple_of(h * half, half), half)

    def load(q):
        return pltpu.make_async_copy(left.at[q], left_v.at[q], lsem.at[q])

    small = [
        pltpu.make_async_copy(start, start_v, lsem.at[S]),
        pltpu.make_async_copy(table, table_v, lsem.at[S + 1]),
    ]

    def shift(q, h):
        return pltpu.make_async_remote_copy(
            src_ref=right.at[q, :, cols(h)], dst_ref=partner.at[q, :, cols(h)],
            send_sem=rs_sem.at[q, h], recv_sem=rr_sem.at[q, h],
            device_id={"bond": behind}, device_id_type=MESH)

    def up(q, h):
        return pltpu.make_async_remote_copy(
            src_ref=pair.at[q, :, cols(h)], dst_ref=below.at[q, :, cols(h)],
            send_sem=ps_sem.at[0, q, h], recv_sem=pr_sem.at[0, q, h],
            device_id={"sec": f + 1}, device_id_type=MESH)

    def down(q, h):
        return pltpu.make_async_remote_copy(
            src_ref=pair.at[q, :, cols(h)], dst_ref=above.at[q, :, cols(h)],
            send_sem=ps_sem.at[1, q, h], recv_sem=pr_sem.at[1, q, h],
            device_id={"sec": f - 1}, device_id_type=MESH)

    def back(s):
        return pltpu.make_async_remote_copy(
            src_ref=out.at[s], dst_ref=right_new.at[s], send_sem=os_sem.at[s],
            recv_sem=or_sem.at[s], device_id={"bond": ahead}, device_id_type=MESH)

    def both(act, where=True):
        @pl.when(jnp.logical_and(where, has_hi))
        def _():
            act(up)

        @pl.when(jnp.logical_and(where, has_lo))
        def _():
            act(down)

    barrier = pltpu.get_barrier_semaphore()
    pl.semaphore_signal(barrier, inc=1, device_id={"bond": ahead}, device_id_type=MESH)
    pl.semaphore_signal(barrier, inc=1, device_id={"bond": behind}, device_id_type=MESH)

    @pl.when(has_lo)
    def _():
        pl.semaphore_signal(barrier, inc=1, device_id={"sec": f - 1}, device_id_type=MESH)

    @pl.when(has_hi)
    def _():
        pl.semaphore_signal(barrier, inc=1, device_id={"sec": f + 1}, device_id_type=MESH)

    for q in range(S):
        load(q).start()
    for copy in small:
        copy.start()
    pl.semaphore_wait(barrier, 2 + has_lo.astype(jnp.int32) + has_hi.astype(jnp.int32))
    for q in range(S):
        for h in range(2):
            shift(q, h).start()

    def multiply(i, c):
        q, h = i // 2, lax.rem(i, 2)

        @pl.when(h == 0)
        def _():
            load(q).wait()

        shift(q, h).wait_recv()
        pair[q, :, cols(h)] = dot(left_v[q], partner[q, :, cols(h)], 1, 0).astype(BF)
        both(lambda way: way(q, h).start(), jnp.logical_or(odd, i < 2 * S - 4))
        return c

    lax.fori_loop(0, 2 * S, multiply, 0)

    @pl.when(jnp.logical_not(has_lo))
    def _():
        below[...] = jnp.zeros_like(below)

    @pl.when(jnp.logical_not(has_hi))
    def _():
        above[...] = jnp.zeros_like(above)

    for copy in small:
        copy.wait()
    for s in range(S):
        bt[s] = start_v[s].T

    firsts = (jnp.maximum(f - 1, 0), f, jnp.minimum(f + 1, nf - 1))
    here = (has_lo.astype(F32), None, has_hi.astype(F32))

    def arrive(q, h):
        @pl.when(has_lo)
        def _():
            up(q, h).wait_recv()

        @pl.when(has_hi)
        def _():
            down(q, h).wait_recv()

    def mix(p, h):
        terms = []
        for first, gone, block in zip(firsts, here, (below, pair, above)):
            for q in range(max(0, p - 1), min(S, p + 2)):
                w = table_v[f * S + p, first * S + q]
                terms.append((w if gone is None else w * gone, block, q))

        def rows(i, c):
            at = pl.ds(pl.multiple_of(i * 32, 32), 32)
            total = None
            for w, block, q in terms:
                term = w * block[q, at, h * half:(h + 1) * half].astype(F32)
                total = term if total is None else total + term
            theta[p, at, h * half:(h + 1) * half] = total.astype(BF)
            return c

        lax.fori_loop(0, d // 32, rows, 0)

    def square(s, h):
        for k in range(2):
            part = slice(k * half, (k + 1) * half)
            wide = slice(h * half, (h + 1) * half)
            o = dot(theta[s, :, wide], theta[s, part, wide], 1, 1)
            if h == 0:
                total[s % 2, :, part] = o
            else:
                hi, lo = split2(total[s % 2, :, part] + o)
                gram[s, 0, :, part] = hi
                gram[s, 1, :, part] = lo

    def by_gram(s, x):
        h, m = split2(x)
        return (sum_rows(dot(jnp.concatenate([h, m], axis=0), gram[s, 0], 1, 0), n)
                + dot(h, gram[s, 1], 1, 0))

    def by_tri(s, x):
        a, b = split2(tri[s * n:(s + 1) * n, :])
        lhs = jnp.concatenate([jnp.concatenate([y, y], axis=1) for y in (a, b)], axis=0)
        return sum_rows(dot(lhs, jnp.concatenate(split2(x), axis=0), 1, 0), n)

    def put(s, g):
        gt[s] = g
        hm = jnp.concatenate(split2(g), axis=0)
        o = dot(hm, hm, 1, 1)
        aug[s * n:(s + 1) * n, :] = (o[:n, :n] + o[n:, n:]) + (o[:n, n:] + o[n:, :n])

    def begin(s):
        for h in range(2):
            mix(s, h)
            square(s, h)
        put(s, by_gram(s, bt[s]))

    for q in range(2):
        for h in range(2):
            arrive(q, h)
    begin(0)

    @pl.when(odd)
    def _():
        for i in range(2 * S):
            if i == 2 * S - 1:
                pl.semaphore_signal(turn, inc=1, device_id={"bond": behind}, device_id_type=MESH)
            both(lambda way: way(i // 2, i % 2).wait_send())

    @pl.when(jnp.logical_not(odd))
    def _():
        pl.semaphore_wait(turn, 1)
        for i in range(2 * S - 4, 2 * S):
            both(lambda way: way(i // 2, i % 2).start())

    for h in range(2):
        arrive(2, h)
    begin(1)
    for h in range(2):
        arrive(3, h)
        for s in (2, 3):
            mix(s, h)
            square(s, h)
    for s in (2, 3):
        put(s, by_gram(s, bt[s]))

    def step(it, c):
        def meanwhile(t):
            if t % 2 == 0 and t // 2 < S:
                ht[t // 2] = by_gram(t // 2, gt[t // 2])

        factor(aug, ubuf, nbuf, tri, n, S, NB, meanwhile)

        @pl.when(it < ITERS - 1)
        def _():
            for s in range(S):
                put(s, by_tri(s, ht[s]))

        return c

    lax.fori_loop(0, ITERS, step, 0)
    row = lax.broadcasted_iota(jnp.int32, (n, d), 0).astype(F32)
    for s in range(S):
        masked = jnp.where(row < table_v[nf * S, s], by_tri(s, gt[s]), 0.0)
        bt[s] = masked
        out[s] = sum_rows(dot(jnp.concatenate(split2(masked), axis=0), theta[s], 1, 0), n).astype(BF)
        back(s).start()
    for s in range(S):
        left_new[s] = bt[s].T.astype(BF)
    for q in range(S):
        for h in range(2):
            shift(q, h).wait_send()
            both(lambda way: way(q, h).wait_send(), jnp.logical_not(odd))

    for s in range(S):
        back(s).wait()


def layer(left, right, table, start):
    S, d, n = start.shape
    block = pltpu.VMEM((S, d, d), BF)
    dma = pltpu.SemaphoreType.DMA
    hbm = pl.BlockSpec(memory_space=pltpu.HBM)
    return pl.pallas_call(
        layer_body,
        out_shape=(jax.ShapeDtypeStruct((S, d, n), BF), jax.ShapeDtypeStruct((S, n, d), BF)),
        in_specs=[hbm] * 4,
        out_specs=[pl.BlockSpec(memory_space=pltpu.VMEM), pl.BlockSpec(memory_space=pl.ANY)],
        scratch_shapes=[block] * 6 + [
            pltpu.VMEM((2, d, d), F32),
            pltpu.VMEM((S, 2, d, d), BF),
            pltpu.VMEM((S, d, n), F32),
            pltpu.SMEM(table.shape, F32),
            pltpu.VMEM((S, n, d), F32),
            pltpu.VMEM((S, n, d), F32),
            pltpu.VMEM((S, n, d), F32),
            pltpu.VMEM((S * n, n), F32),
            pltpu.VMEM((S * NB, n), F32),
            pltpu.VMEM((S * NB, n), F32),
            pltpu.VMEM((S * n, n), F32),
            pltpu.VMEM((S, n, d), BF),
            dma((S + 2,)), dma((S, 2)), dma((S, 2)), dma((2, S, 2)), dma((2, S, 2)), dma((S,)), dma((S,)),
            pltpu.SemaphoreType.REGULAR,
        ],
        compiler_params=pltpu.CompilerParams(
            collective_id=0, has_side_effects=True, vmem_limit_bytes=52 * 2**20),
    )(left, right, table, start)


def shards(left_site, right_site, gate, sign_table, kept, start):
    coef = gate * (1.0 - 2.0 * sign_table.astype(F32))
    counts = jnp.pad(kept.astype(F32), ((0, 0), (0, gate.shape[1] - kept.shape[1])))
    table = jnp.concatenate([coef, counts], axis=0)
    left_new, right_new = layer(left_site[0], right_site[0], table, start[0])
    return left_new[None], right_new[None]


def solution(mesh):
    return jax.shard_map(
        shards,
        mesh=mesh,
        in_specs=(
            P("bond", "sec", None, None),
            P("bond", "sec", None, None),
            P(),
            P(),
            P("bond", "sec"),
            P("bond", "sec", None, None),
        ),
        out_specs=(P("bond", "sec", None, None), P("bond", "sec", None, None)),
        check_vma=False,
    )
```

```python
import jax
import jax.numpy as jnp
from jax import lax
from jax.experimental import pallas as pl
from jax.experimental.pallas import tpu as pltpu
from jax.sharding import PartitionSpec as P

MESH = pl.DeviceIdType.MESH
ITERS = 4
NB = 16
F32=jnp.float32; BF=jnp.bfloat16

def split3(x):
    h=x.astype(BF)
    r=x-h.astype(F32)
    m=r.astype(BF)
    l=(r-m.astype(F32)).astype(BF)
    return h,m,l

def split2(x):
    h = x.astype(BF)
    return h, (x - h.astype(F32)).astype(BF)


def dot(a, b, ca, cb):
    return lax.dot_general(a, b, (((ca,), (cb,)), ((), ())), preferred_element_type=F32)


def factor(aug, ubuf, nbuf, tri, n, S, nb, hook):
    lane = lax.broadcasted_iota(jnp.int32, (2 * S, n), 1)
    lane1 = lax.broadcasted_iota(jnp.int32, (1, n), 1)
    top = nb // 2

    def spread(x, i):
        return jnp.broadcast_to(x[:, i:i + 1], x.shape)

    upper = lax.broadcasted_iota(jnp.int32, (2 * S, n), 0) < S

    def update(z, low, first):
        for k in range(first, top // 2):
            cross = jnp.concatenate([low[k][S:], low[k][:S]], axis=0)
            for p in range(k, top // 2):
                z[p, k] = z[p, k][0] - low[p] * low[k], z[p, k][1] - low[p] * cross

    def dup(x, h):
        part = x[h * S:(h + 1) * S]
        return jnp.concatenate([part, part], axis=0)

    X = [aug[pl.ds(k, S, stride=n), :] for k in range(nb)]
    for t in range(n // nb):
        lo = t * nb
        end = lo + nb
        inside = jnp.logical_and(lane >= lo, lane < end)
        XD = [jnp.concatenate([X[i], X[i]], axis=0) for i in range(top)]
        XP = [jnp.concatenate([X[top + 2 * p], X[top + 2 * p + 1]], axis=0) for p in range(top // 2)]
        v, w, z = {}, {}, {}
        for k in range(top):
            for i in range(k, top):
                v[i, k] = spread(XD[i], lo + k)
            for p in range(top // 2):
                w[p, k] = spread(XP[p], lo + k)
        for k in range(top // 2):
            for p in range(k, top // 2):
                one, two = spread(XP[p], lo + top + 2 * k), spread(XP[p], lo + top + 2 * k + 1)
                z[p, k] = jnp.where(upper, one, two), jnp.where(upper, two, one)
        XD = [jnp.where(inside, 0.0, x) for x in XD]
        XP = [jnp.where(inside, 0.0, x) for x in XP]

        def keep(j, u):
            tri[pl.ds(lo + j, S, stride=n), :] = jnp.where(lane <= lo + j, u, 0.0)[:S]
            if end < n:
                ubuf[pl.ds(j, S, stride=nb), :] = u[:S]

        for j in range(top):
            r = lax.rsqrt(v[j, j])
            u = jnp.where(lane == lo + j, r, XD[j] * r)
            keep(j, u)
            col = {i: v[i, j] * r for i in range(j + 1, top)}
            low = [w[p, j] * r for p in range(top // 2)]
            for i in range(j + 1, top):
                for k in range(j + 1, i + 1):
                    v[i, k] = v[i, k] - col[i] * col[k]
                XD[i] = XD[i] - col[i] * u
            for k in range(j + 1, top):
                for p in range(top // 2):
                    w[p, k] = w[p, k] - low[p] * col[k]
            update(z, low, 0)
            for p in range(top // 2):
                XP[p] = XP[p] - low[p] * u
        for j in range(top):
            q, h = j // 2, j % 2
            r = dup(lax.rsqrt(z[q, q][0]), h)
            u = jnp.where(lane == lo + top + j, r, dup(XP[q], h) * r)
            keep(top + j, u)
            low = {p: jnp.where(upper, z[p, q][h], z[p, q][1 - h]) * r for p in range(q + h, top // 2)}
            update(z, low, q + h)
            for p in low:
                XP[p] = XP[p] - low[p] * u
        if end < n:
            blk = jnp.logical_and(lane1 >= lo, lane1 < end)
            lt, rh = [], []
            for s in range(S):
                h, m, l = split3(ubuf[s * nb:(s + 1) * nb, :])
                lt.append(jnp.concatenate([h, h, m, h, m, l], axis=0).T)
                rh.append(jnp.concatenate([h, m, h, l, m, h], axis=0))
            o = dot(jnp.concatenate([x[end:end + nb] for x in lt], axis=0), jnp.concatenate(rh, axis=1), 1, 0)
            for s in range(S):
                nbuf[s * nb:(s + 1) * nb, :] = (
                    jnp.where(blk, 0.0, aug[s * n + end:s * n + end + nb, :])
                    - o[s * nb:(s + 1) * nb, s * n:(s + 1) * n])
            X = [nbuf[pl.ds(k, S, stride=nb), :] for k in range(nb)]
            hook(t)
            if end + nb < n:
                for s in range(S):
                    rows = slice(s * n + end + nb, (s + 1) * n)
                    aug[rows, :] = jnp.where(blk, 0.0, aug[rows, :]) - dot(lt[s][end + nb:], rh[s], 1, 0)


def sum_rows(x, n):
    total = x[:n]
    for i in range(1, x.shape[0] // n):
        total = total + x[i * n:(i + 1) * n]
    return total


def layer_body(left, right, table, start, left_new, right_new,
               left_v, partner, pair, below, above, theta, total, gram, start_v, table_v,
               bt, gt, ht, aug, ubuf, nbuf, tri, out,
               lsem, rs_sem, rr_sem, ps_sem, pr_sem, os_sem, or_sem, turn):
    S, d, _ = left_v.shape
    n = bt.shape[1]
    bond, bonds = lax.axis_index("bond"), lax.axis_size("bond")
    f, nf = lax.axis_index("sec"), lax.axis_size("sec")
    ahead, behind = lax.rem(bond + 1, bonds), lax.rem(bond + bonds - 1, bonds)
    has_lo, has_hi = f > 0, f < nf - 1
    odd = lax.rem(bond, 2) == 1

    half = d // 2

    def cols(h):
        return pl.ds(pl.multiple_of(h * half, half), half)

    def load(q):
        return pltpu.make_async_copy(left.at[q], left_v.at[q], lsem.at[q])

    small = [
        pltpu.make_async_copy(start, start_v, lsem.at[S]),
        pltpu.make_async_copy(table, table_v, lsem.at[S + 1]),
    ]

    def shift(q, h):
        return pltpu.make_async_remote_copy(
            src_ref=right.at[q, :, cols(h)], dst_ref=partner.at[q, :, cols(h)],
            send_sem=rs_sem.at[q, h], recv_sem=rr_sem.at[q, h],
            device_id={"bond": behind}, device_id_type=MESH)

    def up(q, h):
        return pltpu.make_async_remote_copy(
            src_ref=pair.at[q, :, cols(h)], dst_ref=below.at[q, :, cols(h)],
            send_sem=ps_sem.at[0, q, h], recv_sem=pr_sem.at[0, q, h],
            device_id={"sec": f + 1}, device_id_type=MESH)

    def down(q, h):
        return pltpu.make_async_remote_copy(
            src_ref=pair.at[q, :, cols(h)], dst_ref=above.at[q, :, cols(h)],
            send_sem=ps_sem.at[1, q, h], recv_sem=pr_sem.at[1, q, h],
            device_id={"sec": f - 1}, device_id_type=MESH)

    def back(s):
        return pltpu.make_async_remote_copy(
            src_ref=out.at[s], dst_ref=right_new.at[s], send_sem=os_sem.at[s],
            recv_sem=or_sem.at[s], device_id={"bond": ahead}, device_id_type=MESH)

    def both(act, where=True):
        @pl.when(jnp.logical_and(where, has_hi))
        def _():
            act(up)

        @pl.when(jnp.logical_and(where, has_lo))
        def _():
            act(down)

    barrier = pltpu.get_barrier_semaphore()
    pl.semaphore_signal(barrier, inc=1, device_id={"bond": ahead}, device_id_type=MESH)
    pl.semaphore_signal(barrier, inc=1, device_id={"bond": behind}, device_id_type=MESH)

    @pl.when(has_lo)
    def _():
        pl.semaphore_signal(barrier, inc=1, device_id={"sec": f - 1}, device_id_type=MESH)

    @pl.when(has_hi)
    def _():
        pl.semaphore_signal(barrier, inc=1, device_id={"sec": f + 1}, device_id_type=MESH)

    for q in range(S):
        load(q).start()
    for copy in small:
        copy.start()
    pl.semaphore_wait(barrier, 2 + has_lo.astype(jnp.int32) + has_hi.astype(jnp.int32))
    for q in range(S):
        for h in range(2):
            shift(q, h).start()

    def multiply(i, c):
        q, h = i // 2, lax.rem(i, 2)

        @pl.when(h == 0)
        def _():
            load(q).wait()

        shift(q, h).wait_recv()
        pair[q, :, cols(h)] = dot(left_v[q], partner[q, :, cols(h)], 1, 0).astype(BF)
        both(lambda way: way(q, h).start(), jnp.logical_or(odd, i < 2 * S - 4))
        return c

    lax.fori_loop(0, 2 * S, multiply, 0)

    @pl.when(jnp.logical_not(has_lo))
    def _():
        below[...] = jnp.zeros_like(below)

    @pl.when(jnp.logical_not(has_hi))
    def _():
        above[...] = jnp.zeros_like(above)

    for copy in small:
        copy.wait()
    for s in range(S):
        bt[s] = start_v[s].T

    firsts = (jnp.maximum(f - 1, 0), f, jnp.minimum(f + 1, nf - 1))
    here = (has_lo.astype(F32), None, has_hi.astype(F32))

    def arrive(q, h):
        @pl.when(has_lo)
        def _():
            up(q, h).wait_recv()

        @pl.when(has_hi)
        def _():
            down(q, h).wait_recv()

    def mix(p, h):
        terms = []
        for first, gone, block in zip(firsts, here, (below, pair, above)):
            for q in range(max(0, p - 1), min(S, p + 2)):
                w = table_v[f * S + p, first * S + q]
                terms.append((w if gone is None else w * gone, block, q))

        def rows(i, c):
            at = pl.ds(pl.multiple_of(i * 32, 32), 32)
            total = None
            for w, block, q in terms:
                term = w * block[q, at, h * half:(h + 1) * half].astype(F32)
                total = term if total is None else total + term
            theta[p, at, h * half:(h + 1) * half] = total.astype(BF)
            return c

        lax.fori_loop(0, d // 32, rows, 0)

    def square(s, h):
        for k in range(2):
            part = slice(k * half, (k + 1) * half)
            wide = slice(h * half, (h + 1) * half)
            o = dot(theta[s, :, wide], theta[s, part, wide], 1, 1)
            if h == 0:
                total[s % 2, :, part] = o
            else:
                hi, lo = split2(total[s % 2, :, part] + o)
                gram[s, 0, :, part] = hi
                gram[s, 1, :, part] = lo

    def by_gram(s, x):
        h, m = split2(x)
        return (sum_rows(dot(jnp.concatenate([h, m], axis=0), gram[s, 0], 1, 0), n)
                + dot(h, gram[s, 1], 1, 0))

    def by_tri(s, x):
        a, b = split2(tri[s * n:(s + 1) * n, :])
        lhs = jnp.concatenate([jnp.concatenate([y, y], axis=1) for y in (a, b)], axis=0)
        return sum_rows(dot(lhs, jnp.concatenate(split2(x), axis=0), 1, 0), n)

    def put(s, g):
        gt[s] = g
        hm = jnp.concatenate(split2(g), axis=0)
        o = dot(hm, hm, 1, 1)
        aug[s * n:(s + 1) * n, :] = (o[:n, :n] + o[n:, n:]) + (o[:n, n:] + o[n:, :n])

    def begin(s):
        for h in range(2):
            mix(s, h)
            square(s, h)
        put(s, by_gram(s, bt[s]))

    for q in range(2):
        for h in range(2):
            arrive(q, h)
    begin(0)

    @pl.when(odd)
    def _():
        for i in range(2 * S):
            if i == 2 * S - 1:
                pl.semaphore_signal(turn, inc=1, device_id={"bond": behind}, device_id_type=MESH)
            both(lambda way: way(i // 2, i % 2).wait_send())

    @pl.when(jnp.logical_not(odd))
    def _():
        pl.semaphore_wait(turn, 1)
        for i in range(2 * S - 4, 2 * S):
            both(lambda way: way(i // 2, i % 2).start())

    for h in range(2):
        arrive(2, h)
    begin(1)
    for h in range(2):
        arrive(3, h)
        for s in (2, 3):
            mix(s, h)
            square(s, h)
    for s in (2, 3):
        put(s, by_gram(s, bt[s]))

    def step(it, c):
        def meanwhile(t):
            if t % 2 == 0 and t // 2 < S:
                ht[t // 2] = by_gram(t // 2, gt[t // 2])

        factor(aug, ubuf, nbuf, tri, n, S, NB, meanwhile)

        @pl.when(it < ITERS - 1)
        def _():
            for s in range(S):
                put(s, by_tri(s, ht[s]))

        return c

    lax.fori_loop(0, ITERS, step, 0)
    row = lax.broadcasted_iota(jnp.int32, (n, d), 0).astype(F32)
    for s in range(S):
        masked = jnp.where(row < table_v[nf * S, s], by_tri(s, gt[s]), 0.0)
        bt[s] = masked
        out[s] = sum_rows(dot(jnp.concatenate(split2(masked), axis=0), theta[s], 1, 0), n).astype(BF)
        back(s).start()
    for s in range(S):
        left_new[s] = bt[s].T.astype(BF)
    for q in range(S):
        for h in range(2):
            shift(q, h).wait_send()
            both(lambda way: way(q, h).wait_send(), jnp.logical_not(odd))

    for s in range(S):
        back(s).wait()


def layer(left, right, table, start):
    S, d, n = start.shape
    block = pltpu.VMEM((S, d, d), BF)
    dma = pltpu.SemaphoreType.DMA
    hbm = pl.BlockSpec(memory_space=pltpu.HBM)
    return pl.pallas_call(
        layer_body,
        out_shape=(jax.ShapeDtypeStruct((S, d, n), BF), jax.ShapeDtypeStruct((S, n, d), BF)),
        in_specs=[hbm] * 4,
        out_specs=[pl.BlockSpec(memory_space=pltpu.VMEM), pl.BlockSpec(memory_space=pl.ANY)],
        scratch_shapes=[block] * 6 + [
            pltpu.VMEM((2, d, d), F32),
            pltpu.VMEM((S, 2, d, d), BF),
            pltpu.VMEM((S, d, n), F32),
            pltpu.SMEM(table.shape, F32),
            pltpu.VMEM((S, n, d), F32),
            pltpu.VMEM((S, n, d), F32),
            pltpu.VMEM((S, n, d), F32),
            pltpu.VMEM((S * n, n), F32),
            pltpu.VMEM((S * NB, n), F32),
            pltpu.VMEM((S * NB, n), F32),
            pltpu.VMEM((S * n, n), F32),
            pltpu.VMEM((S, n, d), BF),
            dma((S + 2,)), dma((S, 2)), dma((S, 2)), dma((2, S, 2)), dma((2, S, 2)), dma((S,)), dma((S,)),
            pltpu.SemaphoreType.REGULAR,
        ],
        compiler_params=pltpu.CompilerParams(
            collective_id=0, has_side_effects=True, vmem_limit_bytes=52 * 2**20),
    )(left, right, table, start)


def shards(left_site, right_site, gate, sign_table, kept, start):
    coef = gate * (1.0 - 2.0 * sign_table.astype(F32))
    counts = jnp.pad(kept.astype(F32), ((0, 0), (0, gate.shape[1] - kept.shape[1])))
    table = jnp.concatenate([coef, counts], axis=0)
    left_new, right_new = layer(left_site[0], right_site[0], table, start[0])
    return left_new[None], right_new[None]


def solution(mesh):
    return jax.shard_map(
        shards,
        mesh=mesh,
        in_specs=(
            P("bond", "sec", None, None),
            P("bond", "sec", None, None),
            P(),
            P(),
            P("bond", "sec"),
            P("bond", "sec", None, None),
        ),
        out_specs=(P("bond", "sec", None, None), P("bond", "sec", None, None)),
        check_vma=False,
    )
```

```python
import jax
import jax.numpy as jnp
from jax import lax
from jax.experimental import pallas as pl
from jax.experimental.pallas import tpu as pltpu
from jax.sharding import PartitionSpec as P

MESH = pl.DeviceIdType.MESH
ITERS = 4
NB = 16
F32=jnp.float32; BF=jnp.bfloat16

def split3(x):
    h=x.astype(BF)
    r=x-h.astype(F32)
    m=r.astype(BF)
    l=(r-m.astype(F32)).astype(BF)
    return h,m,l

def split2(x):
    h = x.astype(BF)
    return h, (x - h.astype(F32)).astype(BF)


def dot(a, b, ca, cb):
    return lax.dot_general(a, b, (((ca,), (cb,)), ((), ())), preferred_element_type=F32)


def factor(aug, ubuf, nbuf, tri, n, S, nb, hook):
    lane = lax.broadcasted_iota(jnp.int32, (2 * S, n), 1)
    lane1 = lax.broadcasted_iota(jnp.int32, (1, n), 1)
    top = nb // 2

    def spread(x, i):
        return jnp.broadcast_to(x[:, i:i + 1], x.shape)

    upper = lax.broadcasted_iota(jnp.int32, (2 * S, n), 0) < S

    def update(z, low, first):
        for k in range(first, top // 2):
            cross = jnp.concatenate([low[k][S:], low[k][:S]], axis=0)
            for p in range(k, top // 2):
                z[p, k] = z[p, k][0] - low[p] * low[k], z[p, k][1] - low[p] * cross

    def dup(x, h):
        part = x[h * S:(h + 1) * S]
        return jnp.concatenate([part, part], axis=0)

    X = [aug[pl.ds(k, S, stride=n), :] for k in range(nb)]
    for t in range(n // nb):
        lo = t * nb
        end = lo + nb
        inside = jnp.logical_and(lane >= lo, lane < end)
        XD = [jnp.concatenate([X[i], X[i]], axis=0) for i in range(top)]
        XP = [jnp.concatenate([X[top + 2 * p], X[top + 2 * p + 1]], axis=0) for p in range(top // 2)]
        v, w, z = {}, {}, {}
        for k in range(top):
            for i in range(k, top):
                v[i, k] = spread(XD[i], lo + k)
            for p in range(top // 2):
                w[p, k] = spread(XP[p], lo + k)
        for k in range(top // 2):
            for p in range(k, top // 2):
                one, two = spread(XP[p], lo + top + 2 * k), spread(XP[p], lo + top + 2 * k + 1)
                z[p, k] = jnp.where(upper, one, two), jnp.where(upper, two, one)
        XD = [jnp.where(inside, 0.0, x) for x in XD]
        XP = [jnp.where(inside, 0.0, x) for x in XP]

        def keep(j, u):
            tri[pl.ds(lo + j, S, stride=n), :] = jnp.where(lane <= lo + j, u, 0.0)[:S]
            if end < n:
                ubuf[pl.ds(j, S, stride=nb), :] = u[:S]

        for j in range(top):
            r = lax.rsqrt(v[j, j])
            u = jnp.where(lane == lo + j, r, XD[j] * r)
            keep(j, u)
            col = {i: v[i, j] * r for i in range(j + 1, top)}
            low = [w[p, j] * r for p in range(top // 2)]
            for i in range(j + 1, top):
                for k in range(j + 1, i + 1):
                    v[i, k] = v[i, k] - col[i] * col[k]
                XD[i] = XD[i] - col[i] * u
            for k in range(j + 1, top):
                for p in range(top // 2):
                    w[p, k] = w[p, k] - low[p] * col[k]
            update(z, low, 0)
            for p in range(top // 2):
                XP[p] = XP[p] - low[p] * u
        for j in range(top):
            q, h = j // 2, j % 2
            r = dup(lax.rsqrt(z[q, q][0]), h)
            u = jnp.where(lane == lo + top + j, r, dup(XP[q], h) * r)
            keep(top + j, u)
            low = {p: jnp.where(upper, z[p, q][h], z[p, q][1 - h]) * r for p in range(q + h, top // 2)}
            update(z, low, q + h)
            for p in low:
                XP[p] = XP[p] - low[p] * u
        if end < n:
            blk = jnp.logical_and(lane1 >= lo, lane1 < end)
            lt, rh = [], []
            for s in range(S):
                h, m, l = split3(ubuf[s * nb:(s + 1) * nb, :])
                lt.append(jnp.concatenate([h, h, m, h, m, l], axis=0).T)
                rh.append(jnp.concatenate([h, m, h, l, m, h], axis=0))
            for s in range(S):
                nbuf[s * nb:(s + 1) * nb, :] = (
                    jnp.where(blk, 0.0, aug[s * n + end:s * n + end + nb, :])
                    - dot(lt[s][end:end + nb], rh[s], 1, 0))
            X = [nbuf[pl.ds(k, S, stride=nb), :] for k in range(nb)]
            hook(t)
            if end + nb < n:
                for s in range(S):
                    rows = slice(s * n + end + nb, (s + 1) * n)
                    aug[rows, :] = jnp.where(blk, 0.0, aug[rows, :]) - dot(lt[s][end + nb:], rh[s], 1, 0)


def sum_rows(x, n):
    total = x[:n]
    for i in range(1, x.shape[0] // n):
        total = total + x[i * n:(i + 1) * n]
    return total


def layer_body(left, right, table, start, left_new, right_new,
               left_v, partner, pair, below, above, theta, total, gram, start_v, table_v,
               bt, gt, ht, aug, ubuf, nbuf, tri, out,
               lsem, rs_sem, rr_sem, ps_sem, pr_sem, os_sem, or_sem, turn):
    S, d, _ = left_v.shape
    n = bt.shape[1]
    bond, bonds = lax.axis_index("bond"), lax.axis_size("bond")
    f, nf = lax.axis_index("sec"), lax.axis_size("sec")
    ahead, behind = lax.rem(bond + 1, bonds), lax.rem(bond + bonds - 1, bonds)
    has_lo, has_hi = f > 0, f < nf - 1
    odd = lax.rem(bond, 2) == 1

    half = d // 2

    def cols(h):
        return pl.ds(pl.multiple_of(h * half, half), half)

    def load(q):
        return pltpu.make_async_copy(left.at[q], left_v.at[q], lsem.at[q])

    small = [
        pltpu.make_async_copy(start, start_v, lsem.at[S]),
        pltpu.make_async_copy(table, table_v, lsem.at[S + 1]),
    ]

    def shift(q, h):
        return pltpu.make_async_remote_copy(
            src_ref=right.at[q, :, cols(h)], dst_ref=partner.at[q, :, cols(h)],
            send_sem=rs_sem.at[q, h], recv_sem=rr_sem.at[q, h],
            device_id={"bond": behind}, device_id_type=MESH)

    def up(q, h):
        return pltpu.make_async_remote_copy(
            src_ref=pair.at[q, :, cols(h)], dst_ref=below.at[q, :, cols(h)],
            send_sem=ps_sem.at[0, q, h], recv_sem=pr_sem.at[0, q, h],
            device_id={"sec": f + 1}, device_id_type=MESH)

    def down(q, h):
        return pltpu.make_async_remote_copy(
            src_ref=pair.at[q, :, cols(h)], dst_ref=above.at[q, :, cols(h)],
            send_sem=ps_sem.at[1, q, h], recv_sem=pr_sem.at[1, q, h],
            device_id={"sec": f - 1}, device_id_type=MESH)

    def back(s):
        return pltpu.make_async_remote_copy(
            src_ref=out.at[s], dst_ref=right_new.at[s], send_sem=os_sem.at[s],
            recv_sem=or_sem.at[s], device_id={"bond": ahead}, device_id_type=MESH)

    def both(act, where=True):
        @pl.when(jnp.logical_and(where, has_hi))
        def _():
            act(up)

        @pl.when(jnp.logical_and(where, has_lo))
        def _():
            act(down)

    barrier = pltpu.get_barrier_semaphore()
    pl.semaphore_signal(barrier, inc=1, device_id={"bond": ahead}, device_id_type=MESH)
    pl.semaphore_signal(barrier, inc=1, device_id={"bond": behind}, device_id_type=MESH)

    @pl.when(has_lo)
    def _():
        pl.semaphore_signal(barrier, inc=1, device_id={"sec": f - 1}, device_id_type=MESH)

    @pl.when(has_hi)
    def _():
        pl.semaphore_signal(barrier, inc=1, device_id={"sec": f + 1}, device_id_type=MESH)

    for q in range(S):
        load(q).start()
    for copy in small:
        copy.start()
    pl.semaphore_wait(barrier, 2 + has_lo.astype(jnp.int32) + has_hi.astype(jnp.int32))
    for q in range(S):
        for h in range(2):
            shift(q, h).start()

    def multiply(i, c):
        q, h = i // 2, lax.rem(i, 2)

        @pl.when(h == 0)
        def _():
            load(q).wait()

        shift(q, h).wait_recv()
        pair[q, :, cols(h)] = dot(left_v[q], partner[q, :, cols(h)], 1, 0).astype(BF)
        both(lambda way: way(q, h).start(), jnp.logical_or(odd, i < 2 * S - 4))
        return c

    lax.fori_loop(0, 2 * S, multiply, 0)

    @pl.when(jnp.logical_not(has_lo))
    def _():
        below[...] = jnp.zeros_like(below)

    @pl.when(jnp.logical_not(has_hi))
    def _():
        above[...] = jnp.zeros_like(above)

    for copy in small:
        copy.wait()
    for s in range(S):
        bt[s] = start_v[s].T

    firsts = (jnp.maximum(f - 1, 0), f, jnp.minimum(f + 1, nf - 1))
    here = (has_lo.astype(F32), None, has_hi.astype(F32))

    def arrive(q, h):
        @pl.when(has_lo)
        def _():
            up(q, h).wait_recv()

        @pl.when(has_hi)
        def _():
            down(q, h).wait_recv()

    def mix(p, h):
        terms = []
        for first, gone, block in zip(firsts, here, (below, pair, above)):
            for q in range(max(0, p - 1), min(S, p + 2)):
                w = table_v[f * S + p, first * S + q]
                terms.append((w if gone is None else w * gone, block, q))

        def rows(i, c):
            at = pl.ds(pl.multiple_of(i * 32, 32), 32)
            total = None
            for w, block, q in terms:
                term = w * block[q, at, h * half:(h + 1) * half].astype(F32)
                total = term if total is None else total + term
            theta[p, at, h * half:(h + 1) * half] = total.astype(BF)
            return c

        lax.fori_loop(0, d // 32, rows, 0)

    def square(s, h):
        for k in range(2):
            part = slice(k * half, (k + 1) * half)
            wide = slice(h * half, (h + 1) * half)
            o = dot(theta[s, :, wide], theta[s, part, wide], 1, 1)
            if h == 0:
                total[s % 2, :, part] = o
            else:
                hi, lo = split2(total[s % 2, :, part] + o)
                gram[s, 0, :, part] = hi
                gram[s, 1, :, part] = lo

    def by_gram(s, x):
        h, m = split2(x)
        return (sum_rows(dot(jnp.concatenate([h, m], axis=0), gram[s, 0], 1, 0), n)
                + dot(h, gram[s, 1], 1, 0))

    def by_tri(s, x):
        a, b = split2(tri[s * n:(s + 1) * n, :])
        lhs = jnp.concatenate([jnp.concatenate([y, y], axis=1) for y in (a, b)], axis=0)
        return sum_rows(dot(lhs, jnp.concatenate(split2(x), axis=0), 1, 0), n)

    def put(s, g):
        gt[s] = g
        hm = jnp.concatenate(split2(g), axis=0)
        o = dot(hm, hm, 1, 1)
        aug[s * n:(s + 1) * n, :] = (o[:n, :n] + o[n:, n:]) + (o[:n, n:] + o[n:, :n])

    def begin(s):
        for h in range(2):
            mix(s, h)
            square(s, h)
        put(s, by_gram(s, bt[s]))

    for q in range(2):
        for h in range(2):
            arrive(q, h)
    begin(0)

    @pl.when(odd)
    def _():
        for i in range(2 * S):
            if i == 2 * S - 1:
                pl.semaphore_signal(turn, inc=1, device_id={"bond": behind}, device_id_type=MESH)
            both(lambda way: way(i // 2, i % 2).wait_send())

    @pl.when(jnp.logical_not(odd))
    def _():
        pl.semaphore_wait(turn, 1)
        for i in range(2 * S - 4, 2 * S):
            both(lambda way: way(i // 2, i % 2).start())

    for h in range(2):
        arrive(2, h)
    begin(1)
    for h in range(2):
        arrive(3, h)
        for s in (2, 3):
            mix(s, h)
            square(s, h)
    for s in (2, 3):
        put(s, by_gram(s, bt[s]))

    def step(it, c):
        def meanwhile(t):
            if t % 2 == 0 and t // 2 < S:
                ht[t // 2] = by_gram(t // 2, gt[t // 2])

        factor(aug, ubuf, nbuf, tri, n, S, NB, meanwhile)

        @pl.when(it < ITERS - 1)
        def _():
            for s in range(S):
                put(s, by_tri(s, ht[s]))

        return c

    lax.fori_loop(0, ITERS, step, 0)
    row = lax.broadcasted_iota(jnp.int32, (n, d), 0).astype(F32)
    for s in range(S):
        masked = jnp.where(row < table_v[nf * S, s], by_tri(s, gt[s]), 0.0)
        bt[s] = masked
        out[s] = sum_rows(dot(jnp.concatenate(split2(masked), axis=0), theta[s], 1, 0), n).astype(BF)
        back(s).start()
    for s in range(S):
        left_new[s] = bt[s].T.astype(BF)
    for q in range(S):
        for h in range(2):
            shift(q, h).wait_send()
            both(lambda way: way(q, h).wait_send(), jnp.logical_not(odd))

    for s in range(S):
        back(s).wait()


def layer(left, right, table, start):
    S, d, n = start.shape
    block = pltpu.VMEM((S, d, d), BF)
    dma = pltpu.SemaphoreType.DMA
    hbm = pl.BlockSpec(memory_space=pltpu.HBM)
    return pl.pallas_call(
        layer_body,
        out_shape=(jax.ShapeDtypeStruct((S, d, n), BF), jax.ShapeDtypeStruct((S, n, d), BF)),
        in_specs=[hbm] * 4,
        out_specs=[pl.BlockSpec(memory_space=pltpu.VMEM), pl.BlockSpec(memory_space=pl.ANY)],
        scratch_shapes=[block] * 6 + [
            pltpu.VMEM((2, d, d), F32),
            pltpu.VMEM((S, 2, d, d), BF),
            pltpu.VMEM((S, d, n), F32),
            pltpu.SMEM(table.shape, F32),
            pltpu.VMEM((S, n, d), F32),
            pltpu.VMEM((S, n, d), F32),
            pltpu.VMEM((S, n, d), F32),
            pltpu.VMEM((S * n, n), F32),
            pltpu.VMEM((S * NB, n), F32),
            pltpu.VMEM((S * NB, n), F32),
            pltpu.VMEM((S * n, n), F32),
            pltpu.VMEM((S, n, d), BF),
            dma((S + 2,)), dma((S, 2)), dma((S, 2)), dma((2, S, 2)), dma((2, S, 2)), dma((S,)), dma((S,)),
            pltpu.SemaphoreType.REGULAR,
        ],
        compiler_params=pltpu.CompilerParams(
            collective_id=0, has_side_effects=True, vmem_limit_bytes=52 * 2**20),
    )(left, right, table, start)


def shards(left_site, right_site, gate, sign_table, kept, start):
    coef = gate * (1.0 - 2.0 * sign_table.astype(F32))
    counts = jnp.pad(kept.astype(F32), ((0, 0), (0, gate.shape[1] - kept.shape[1])))
    table = jnp.concatenate([coef, counts], axis=0)
    left_new, right_new = layer(left_site[0], right_site[0], table, start[0])
    return left_new[None], right_new[None]


def solution(mesh):
    return jax.shard_map(
        shards,
        mesh=mesh,
        in_specs=(
            P("bond", "sec", None, None),
            P("bond", "sec", None, None),
            P(),
            P(),
            P("bond", "sec"),
            P("bond", "sec", None, None),
        ),
        out_specs=(P("bond", "sec", None, None), P("bond", "sec", None, None)),
        check_vma=False,
    )
```

```python
import jax
import jax.numpy as jnp
from jax import lax
from jax.experimental import pallas as pl
from jax.experimental.pallas import tpu as pltpu
from jax.sharding import PartitionSpec as P

MESH = pl.DeviceIdType.MESH
ITERS = 4
NB = 16
F32=jnp.float32; BF=jnp.bfloat16

def split3(x):
    h=x.astype(BF)
    r=x-h.astype(F32)
    m=r.astype(BF)
    l=(r-m.astype(F32)).astype(BF)
    return h,m,l

def split2(x):
    h = x.astype(BF)
    return h, (x - h.astype(F32)).astype(BF)


def dot(a, b, ca, cb):
    return lax.dot_general(a, b, (((ca,), (cb,)), ((), ())), preferred_element_type=F32)


def factor(aug, ubuf, nbuf, tri, n, S, nb, hook):
    lane = lax.broadcasted_iota(jnp.int32, (2 * S, n), 1)
    lane1 = lax.broadcasted_iota(jnp.int32, (1, n), 1)
    top = nb // 2

    def spread(x, i):
        return jnp.broadcast_to(x[:, i:i + 1], x.shape)

    upper = lax.broadcasted_iota(jnp.int32, (2 * S, n), 0) < S

    def update(z, low, first):
        for k in range(first, top // 2):
            cross = jnp.concatenate([low[k][S:], low[k][:S]], axis=0)
            for p in range(k, top // 2):
                z[p, k] = z[p, k][0] - low[p] * low[k], z[p, k][1] - low[p] * cross

    def dup(x, h):
        part = x[h * S:(h + 1) * S]
        return jnp.concatenate([part, part], axis=0)

    X = [aug[pl.ds(k, S, stride=n), :] for k in range(nb)]
    for t in range(n // nb):
        lo = t * nb
        end = lo + nb
        inside = jnp.logical_and(lane >= lo, lane < end)
        XD = [jnp.concatenate([X[i], X[i]], axis=0) for i in range(top)]
        XP = [jnp.concatenate([X[top + 2 * p], X[top + 2 * p + 1]], axis=0) for p in range(top // 2)]
        v, w, z = {}, {}, {}
        for k in range(top):
            for i in range(k, top):
                v[i, k] = spread(XD[i], lo + k)
            for p in range(top // 2):
                w[p, k] = spread(XP[p], lo + k)
        for k in range(top // 2):
            for p in range(k, top // 2):
                one, two = spread(XP[p], lo + top + 2 * k), spread(XP[p], lo + top + 2 * k + 1)
                z[p, k] = jnp.where(upper, one, two), jnp.where(upper, two, one)
        XD = [jnp.where(inside, 0.0, x) for x in XD]
        XP = [jnp.where(inside, 0.0, x) for x in XP]

        def keep(j, u):
            tri[pl.ds(lo + j, S, stride=n), :] = jnp.where(lane <= lo + j, u, 0.0)[:S]
            if end < n:
                ubuf[pl.ds(j, S, stride=nb), :] = u[:S]

        for j in range(top):
            r = lax.rsqrt(v[j, j])
            u = jnp.where(lane == lo + j, r, XD[j] * r)
            keep(j, u)
            col = {i: v[i, j] * r for i in range(j + 1, top)}
            low = [w[p, j] * r for p in range(top // 2)]
            for i in range(j + 1, top):
                for k in range(j + 1, i + 1):
                    v[i, k] = v[i, k] - col[i] * col[k]
                XD[i] = XD[i] - col[i] * u
            for k in range(j + 1, top):
                for p in range(top // 2):
                    w[p, k] = w[p, k] - low[p] * col[k]
            update(z, low, 0)
            for p in range(top // 2):
                XP[p] = XP[p] - low[p] * u
        for j in range(top):
            q, h = j // 2, j % 2
            r = dup(lax.rsqrt(z[q, q][0]), h)
            u = jnp.where(lane == lo + top + j, r, dup(XP[q], h) * r)
            keep(top + j, u)
            low = {p: jnp.where(upper, z[p, q][h], z[p, q][1 - h]) * r for p in range(q + h, top // 2)}
            update(z, low, q + h)
            for p in low:
                XP[p] = XP[p] - low[p] * u
        if end < n:
            blk = jnp.logical_and(lane1 >= lo, lane1 < end)
            lt, rh = [], []
            for s in range(S):
                h, m, l = split3(ubuf[s * nb:(s + 1) * nb, :])
                lt.append(jnp.concatenate([h, h, m, h, m, l], axis=0).T)
                rh.append(jnp.concatenate([h, m, h, l, m, h], axis=0))
            for s in range(S):
                nbuf[s * nb:(s + 1) * nb, :] = (
                    jnp.where(blk, 0.0, aug[s * n + end:s * n + end + nb, :])
                    - dot(lt[s][end:end + nb], rh[s], 1, 0))
            X = [nbuf[pl.ds(k, S, stride=nb), :] for k in range(nb)]
            hook(t)
            if end + nb < n:
                for s in range(S):
                    rows = slice(s * n + end + nb, (s + 1) * n)
                    aug[rows, :] = jnp.where(blk, 0.0, aug[rows, :]) - dot(lt[s][end + nb:], rh[s], 1, 0)


def sum_rows(x, n):
    total = x[:n]
    for i in range(1, x.shape[0] // n):
        total = total + x[i * n:(i + 1) * n]
    return total


def layer_body(left, right, table, start, left_new, right_new,
               left_v, partner, pair, below, above, theta, partial, total, gram, start_v, table_v,
               bt, gt, ht, aug, ubuf, nbuf, tri, out,
               lsem, rs_sem, rr_sem, ps_sem, pr_sem, os_sem, or_sem, turn):
    S, d, _ = left_v.shape
    n = bt.shape[1]
    bond, bonds = lax.axis_index("bond"), lax.axis_size("bond")
    f, nf = lax.axis_index("sec"), lax.axis_size("sec")
    ahead, behind = lax.rem(bond + 1, bonds), lax.rem(bond + bonds - 1, bonds)
    has_lo, has_hi = f > 0, f < nf - 1
    odd = lax.rem(bond, 2) == 1

    half = d // 2

    def cols(h):
        return pl.ds(pl.multiple_of(h * half, half), half)

    def load(q):
        return pltpu.make_async_copy(left.at[q], left_v.at[q], lsem.at[q])

    small = [
        pltpu.make_async_copy(start, start_v, lsem.at[S]),
        pltpu.make_async_copy(table, table_v, lsem.at[S + 1]),
    ]

    def shift(q, h):
        return pltpu.make_async_remote_copy(
            src_ref=right.at[q, :, cols(h)], dst_ref=partner.at[q, :, cols(h)],
            send_sem=rs_sem.at[q, h], recv_sem=rr_sem.at[q, h],
            device_id={"bond": behind}, device_id_type=MESH)

    def up(q, h):
        return pltpu.make_async_remote_copy(
            src_ref=pair.at[q, :, cols(h)], dst_ref=below.at[q, :, cols(h)],
            send_sem=ps_sem.at[0, q, h], recv_sem=pr_sem.at[0, q, h],
            device_id={"sec": f + 1}, device_id_type=MESH)

    def down(q, h):
        return pltpu.make_async_remote_copy(
            src_ref=pair.at[q, :, cols(h)], dst_ref=above.at[q, :, cols(h)],
            send_sem=ps_sem.at[1, q, h], recv_sem=pr_sem.at[1, q, h],
            device_id={"sec": f - 1}, device_id_type=MESH)

    def back(s):
        return pltpu.make_async_remote_copy(
            src_ref=out.at[s], dst_ref=right_new.at[s], send_sem=os_sem.at[s],
            recv_sem=or_sem.at[s], device_id={"bond": ahead}, device_id_type=MESH)

    def both(act, where=True):
        @pl.when(jnp.logical_and(where, has_hi))
        def _():
            act(up)

        @pl.when(jnp.logical_and(where, has_lo))
        def _():
            act(down)

    barrier = pltpu.get_barrier_semaphore()
    pl.semaphore_signal(barrier, inc=1, device_id={"bond": ahead}, device_id_type=MESH)
    pl.semaphore_signal(barrier, inc=1, device_id={"bond": behind}, device_id_type=MESH)

    @pl.when(has_lo)
    def _():
        pl.semaphore_signal(barrier, inc=1, device_id={"sec": f - 1}, device_id_type=MESH)

    @pl.when(has_hi)
    def _():
        pl.semaphore_signal(barrier, inc=1, device_id={"sec": f + 1}, device_id_type=MESH)

    for q in range(S):
        load(q).start()
    for copy in small:
        copy.start()
    pl.semaphore_wait(barrier, 2 + has_lo.astype(jnp.int32) + has_hi.astype(jnp.int32))
    for q in range(S):
        for h in range(2):
            shift(q, h).start()

    def multiply(i, c):
        q, h = i // 2, lax.rem(i, 2)

        @pl.when(h == 0)
        def _():
            load(q).wait()

        shift(q, h).wait_recv()
        pair[q, :, cols(h)] = dot(left_v[q], partner[q, :, cols(h)], 1, 0).astype(BF)
        both(lambda way: way(q, h).start(), jnp.logical_or(odd, i < 2 * S - 4))
        return c

    lax.fori_loop(0, 2 * S, multiply, 0)

    @pl.when(jnp.logical_not(has_lo))
    def _():
        below[...] = jnp.zeros_like(below)

    @pl.when(jnp.logical_not(has_hi))
    def _():
        above[...] = jnp.zeros_like(above)

    for copy in small:
        copy.wait()
    for s in range(S):
        bt[s] = start_v[s].T

    firsts = (jnp.maximum(f - 1, 0), f, jnp.minimum(f + 1, nf - 1))
    here = (has_lo.astype(F32), None, has_hi.astype(F32))

    def arrive(q, h):
        @pl.when(has_lo)
        def _():
            up(q, h).wait_recv()

        @pl.when(has_hi)
        def _():
            down(q, h).wait_recv()

    def mix(p, h, early=False, late=False):
        terms = []
        for first, gone, block in zip(firsts, here, (below, pair, above)):
            for q in range(max(0, p - 1), min(S, p + 2)):
                last = q == S - 1 and gone is not None
                if (early and last) or (late and not last):
                    continue
                w = table_v[f * S + p, first * S + q]
                terms.append((w if gone is None else w * gone, block, q))
        wide = slice(h * half, (h + 1) * half)

        def rows(i, c):
            at = pl.ds(pl.multiple_of(i * 32, 32), 32)
            value = partial[p % 2, at, wide] if late else None
            for w, block, q in terms:
                term = w * block[q, at, wide].astype(F32)
                value = term if value is None else value + term
            if early:
                partial[p % 2, at, wide] = value
            else:
                theta[p, at, wide] = value.astype(BF)
            return c

        lax.fori_loop(0, d // 32, rows, 0)

    def square(s, h):
        for k in range(2):
            part = slice(k * half, (k + 1) * half)
            wide = slice(h * half, (h + 1) * half)
            o = dot(theta[s, :, wide], theta[s, part, wide], 1, 1)
            if h == 0:
                total[s % 2, :, part] = o
            else:
                hi, lo = split2(total[s % 2, :, part] + o)
                gram[s, 0, :, part] = hi
                gram[s, 1, :, part] = lo

    def by_gram(s, x):
        h, m = split2(x)
        return (sum_rows(dot(jnp.concatenate([h, m], axis=0), gram[s, 0], 1, 0), n)
                + dot(h, gram[s, 1], 1, 0))

    def by_tri(s, x):
        a, b = split2(tri[s * n:(s + 1) * n, :])
        lhs = jnp.concatenate([jnp.concatenate([y, y], axis=1) for y in (a, b)], axis=0)
        return sum_rows(dot(lhs, jnp.concatenate(split2(x), axis=0), 1, 0), n)

    def put(s, g):
        gt[s] = g
        hm = jnp.concatenate(split2(g), axis=0)
        o = dot(hm, hm, 1, 1)
        aug[s * n:(s + 1) * n, :] = (o[:n, :n] + o[n:, n:]) + (o[:n, n:] + o[n:, :n])

    def begin(s):
        for h in range(2):
            mix(s, h)
            square(s, h)
        put(s, by_gram(s, bt[s]))

    for q in range(2):
        for h in range(2):
            arrive(q, h)
    begin(0)

    @pl.when(odd)
    def _():
        for i in range(2 * S):
            if i == 2 * S - 1:
                pl.semaphore_signal(turn, inc=1, device_id={"bond": behind}, device_id_type=MESH)
            both(lambda way: way(i // 2, i % 2).wait_send())

    @pl.when(jnp.logical_not(odd))
    def _():
        pl.semaphore_wait(turn, 1)
        for i in range(2 * S - 4, 2 * S):
            both(lambda way: way(i // 2, i % 2).start())

    for h in range(2):
        arrive(2, h)
    begin(1)
    for h in range(2):
        for s in (2, 3):
            mix(s, h, early=True)
    for h in range(2):
        arrive(3, h)
        for s in (2, 3):
            mix(s, h, late=True)
            square(s, h)
    for s in (2, 3):
        put(s, by_gram(s, bt[s]))

    def step(it, c):
        def meanwhile(t):
            if t % 2 == 0 and t // 2 < S:
                ht[t // 2] = by_gram(t // 2, gt[t // 2])

        factor(aug, ubuf, nbuf, tri, n, S, NB, meanwhile)

        @pl.when(it < ITERS - 1)
        def _():
            for s in range(S):
                put(s, by_tri(s, ht[s]))

        return c

    lax.fori_loop(0, ITERS, step, 0)
    row = lax.broadcasted_iota(jnp.int32, (n, d), 0).astype(F32)
    for s in range(S):
        masked = jnp.where(row < table_v[nf * S, s], by_tri(s, gt[s]), 0.0)
        bt[s] = masked
        out[s] = sum_rows(dot(jnp.concatenate(split2(masked), axis=0), theta[s], 1, 0), n).astype(BF)
        back(s).start()
    for s in range(S):
        left_new[s] = bt[s].T.astype(BF)
    for q in range(S):
        for h in range(2):
            shift(q, h).wait_send()
            both(lambda way: way(q, h).wait_send(), jnp.logical_not(odd))

    for s in range(S):
        back(s).wait()


def layer(left, right, table, start):
    S, d, n = start.shape
    block = pltpu.VMEM((S, d, d), BF)
    dma = pltpu.SemaphoreType.DMA
    hbm = pl.BlockSpec(memory_space=pltpu.HBM)
    return pl.pallas_call(
        layer_body,
        out_shape=(jax.ShapeDtypeStruct((S, d, n), BF), jax.ShapeDtypeStruct((S, n, d), BF)),
        in_specs=[hbm] * 4,
        out_specs=[pl.BlockSpec(memory_space=pltpu.VMEM), pl.BlockSpec(memory_space=pl.ANY)],
        scratch_shapes=[block] * 6 + [
            pltpu.VMEM((2, d, d), F32),
            pltpu.VMEM((2, d, d), F32),
            pltpu.VMEM((S, 2, d, d), BF),
            pltpu.VMEM((S, d, n), F32),
            pltpu.SMEM(table.shape, F32),
            pltpu.VMEM((S, n, d), F32),
            pltpu.VMEM((S, n, d), F32),
            pltpu.VMEM((S, n, d), F32),
            pltpu.VMEM((S * n, n), F32),
            pltpu.VMEM((S * NB, n), F32),
            pltpu.VMEM((S * NB, n), F32),
            pltpu.VMEM((S * n, n), F32),
            pltpu.VMEM((S, n, d), BF),
            dma((S + 2,)), dma((S, 2)), dma((S, 2)), dma((2, S, 2)), dma((2, S, 2)), dma((S,)), dma((S,)),
            pltpu.SemaphoreType.REGULAR,
        ],
        compiler_params=pltpu.CompilerParams(
            collective_id=0, has_side_effects=True, vmem_limit_bytes=52 * 2**20),
    )(left, right, table, start)


def shards(left_site, right_site, gate, sign_table, kept, start):
    coef = gate * (1.0 - 2.0 * sign_table.astype(F32))
    counts = jnp.pad(kept.astype(F32), ((0, 0), (0, gate.shape[1] - kept.shape[1])))
    table = jnp.concatenate([coef, counts], axis=0)
    left_new, right_new = layer(left_site[0], right_site[0], table, start[0])
    return left_new[None], right_new[None]


def solution(mesh):
    return jax.shard_map(
        shards,
        mesh=mesh,
        in_specs=(
            P("bond", "sec", None, None),
            P("bond", "sec", None, None),
            P(),
            P(),
            P("bond", "sec"),
            P("bond", "sec", None, None),
        ),
        out_specs=(P("bond", "sec", None, None), P("bond", "sec", None, None)),
        check_vma=False,
    )
```
